32 devices in a mesh: ctx: 16 (over z, y, x), dp: 2 (over core).
Axes of the slice: x: 2, y: 2, z: 4, core: 2. Of those that a mesh axis runs over, the one named last changes fastest.
Arguments:
- normed_input: bfloat16 [2, 2048, 4096], P('dp', 'ctx'), may hold values from -6 to 6
- projection_output_gradient: bfloat16 [2, 2048, 4096], P('dp', 'ctx'), may hold values from -1 to 1
- query: bfloat16 [2, 2048, 2048], P('dp', 'ctx'), may hold values from -5 to 5
- key: bfloat16 [2, 2048, 2048], P('dp', 'ctx'), may hold values from -5 to 5
- value: bfloat16 [2, 2048, 2048], P('dp', 'ctx'), may hold values from -5 to 5
- frozen_output_gradient: bfloat16 [2, 2048, 2048], P('dp', 'ctx'), may hold values from -1 to 1
- query_down_weight: bfloat16 [4096, 8], replicated, may hold values from -0.09375 to 0.09375
- query_up_weight: bfloat16 [8, 2048], replicated, may hold values from -2 to 2
- key_down_weight: bfloat16 [4096, 8], replicated, may hold values from -0.09375 to 0.09375
- key_up_weight: bfloat16 [8, 2048], replicated, may hold values from -2 to 2
- value_down_weight: bfloat16 [4096, 8], replicated, may hold values from -0.09375 to 0.09375
- value_up_weight: bfloat16 [8, 2048], replicated, may hold values from -2 to 2
- output_down_weight: bfloat16 [2048, 8], replicated, may hold values from -2 to 2
- output_up_weight: bfloat16 [8, 4096], replicated, may hold values from -2 to 2
Outputs:
- grad_a_query: float32 [4096, 8], replicated
- grad_b_query: float32 [8, 2048], replicated
- grad_a_key: float32 [4096, 8], replicated
- grad_b_key: float32 [8, 2048], replicated
- grad_a_value: float32 [4096, 8], replicated
- grad_b_value: float32 [8, 2048], replicated
- grad_a_out: float32 [2048, 8], replicated
- grad_b_out: float32 [8, 4096], replicated
The draws below stay inside these ranges and needn't reach their ends.
All inputs are finite; a program needn't handle non-finite values.
Results may differ from the reference program's by a relative error of at most 0.012.
Values may be sent and summed in bfloat16 or wider, within the bound.
No kernel may reach another device: no remote copies, remote signals or barrier semaphores. Data moves between devices by JAX's collectives and lax.ppermute only.
A program may use at most 128 MiB of HBM per device.

```python
import jax
import jax.numpy as jnp
from jax import lax

MODEL_WIDTH = 4096
SHIFT_HEADS = 16
HEAD_WIDTH = 128
ADAPTER_RANK = 8
GROUP = 2048
SEQ_LEN = 2048
SEQS = 2


def draw_query(key, part):
    key = jax.random.fold_in(key, 11)
    entries = jnp.clip(jax.random.normal(key, (SEQS, SEQ_LEN, SHIFT_HEADS * HEAD_WIDTH), jnp.float32), -5.0, 5.0)
    return entries.astype(jnp.bfloat16)


def draw_key(key, part):
    key = jax.random.fold_in(key, 23)
    entries = jnp.clip(jax.random.normal(key, (SEQS, SEQ_LEN, SHIFT_HEADS * HEAD_WIDTH), jnp.float32), -5.0, 5.0)
    return entries.astype(jnp.bfloat16)


def levels(key, extent, cuts, least, largest):
    factor_of, own = 1.0, jax.random.fold_in(key, 6)
    for dim, shards_of in cuts:
        draws = jnp.exp(jax.random.uniform(jax.random.fold_in(own, dim), (shards_of,), jnp.float32, least / len(cuts), largest / len(cuts)))
        factor_of = factor_of * jnp.repeat(draws, extent[dim] // shards_of).reshape([-1 if axis == dim else 1 for axis in range(len(extent))])
    return factor_of


def noise(key, extent, scale, most, cuts=(), held_as=jnp.bfloat16):
    gain = levels(key, extent, cuts, -0.22, 0.18) if cuts else 1.0
    result = jax.random.normal(key, extent, jnp.float32) * scale * gain
    return jnp.minimum(jnp.maximum(result, -most), most).astype(held_as)


def setup_inputs(seed: int = 0) -> dict:
    key_of = jax.random.split(jax.random.key(seed), 15)
    normed_input = noise(key_of[0], (SEQS, SEQ_LEN, MODEL_WIDTH), 1.0, 6.0, ((0, 2), (1, 16)))
    projection_output_gradient = noise(key_of[1], (SEQS, SEQ_LEN, MODEL_WIDTH), (4.0 / (SEQS * SEQ_LEN) ** 0.5), 1.0, ((0, 2), (1, 16)))
    query = draw_query(jax.random.fold_in(key_of[14], 71), 0)
    key = draw_key(jax.random.fold_in(key_of[14], 71), 0)
    value = noise(key_of[4], (SEQS, SEQ_LEN, SHIFT_HEADS * HEAD_WIDTH), 1.0, 5.0, ((0, 2), (1, 16)))
    frozen_output_gradient = noise(key_of[5], (SEQS, SEQ_LEN, SHIFT_HEADS * HEAD_WIDTH), (4.0 / (SEQS * SEQ_LEN) ** 0.5), 1.0, ((0, 2), (1, 16)))
    query_down_weight = noise(key_of[6], (MODEL_WIDTH, ADAPTER_RANK), MODEL_WIDTH ** -0.5, 0.09375)
    query_up_weight = noise(key_of[7], (ADAPTER_RANK, SHIFT_HEADS * HEAD_WIDTH), ADAPTER_RANK ** -0.5, 2.0)
    key_down_weight = noise(key_of[8], (MODEL_WIDTH, ADAPTER_RANK), MODEL_WIDTH ** -0.5, 0.09375)
    key_up_weight = noise(key_of[9], (ADAPTER_RANK, SHIFT_HEADS * HEAD_WIDTH), ADAPTER_RANK ** -0.5, 2.0)
    value_down_weight = noise(key_of[10], (MODEL_WIDTH, ADAPTER_RANK), MODEL_WIDTH ** -0.5, 0.09375)
    value_up_weight = noise(key_of[11], (ADAPTER_RANK, SHIFT_HEADS * HEAD_WIDTH), ADAPTER_RANK ** -0.5, 2.0)
    output_down_weight = noise(key_of[12], (SHIFT_HEADS * HEAD_WIDTH, ADAPTER_RANK), ADAPTER_RANK ** -0.5, 2.0)
    output_up_weight = noise(key_of[13], (ADAPTER_RANK, MODEL_WIDTH), ADAPTER_RANK ** -0.5, 2.0)
    return dict(normed_input=normed_input, projection_output_gradient=projection_output_gradient, query=query, key=key, value=value, frozen_output_gradient=frozen_output_gradient, query_down_weight=query_down_weight, query_up_weight=query_up_weight, key_down_weight=key_down_weight, key_up_weight=key_up_weight, value_down_weight=value_down_weight, value_up_weight=value_up_weight, output_down_weight=output_down_weight, output_up_weight=output_up_weight)


masked_score = -1e30


def head_terms(queries, grads, keys, values, key_low, value_low, key_up, value_up, allowed):
    scale = HEAD_WIDTH ** -0.5
    scores = jnp.dot(queries, keys.T, preferred_element_type=jnp.float32) * scale
    scores = jnp.where(allowed > 0, scores, masked_score)
    summit = jnp.max(scores, axis=-1, keepdims=True)
    weights = jnp.exp(scores - summit)
    weights = weights / jnp.sum(weights, axis=-1, keepdims=True)
    rounded = weights.astype(jnp.bfloat16)
    output = jnp.dot(rounded, values, preferred_element_type=jnp.float32)
    delta = jnp.sum(grads.astype(jnp.float32) * output, axis=-1, keepdims=True)
    dweights = jnp.dot(grads, values.T, preferred_element_type=jnp.float32)
    dscores = (scale * weights * (dweights - delta)).astype(jnp.bfloat16)
    query_gradient = jnp.dot(dscores, keys, preferred_element_type=jnp.float32).astype(jnp.bfloat16)
    query_proj = jnp.dot(queries, key_up.T, preferred_element_type=jnp.float32).astype(jnp.bfloat16)
    grad_proj = jnp.dot(grads, value_up.T, preferred_element_type=jnp.float32).astype(jnp.bfloat16)
    key_terms = jnp.dot(dscores.T, query_proj, preferred_element_type=jnp.float32)
    value_terms = jnp.dot(rounded.T, grad_proj, preferred_element_type=jnp.float32)
    key_mix = jnp.dot(dscores, key_low, preferred_element_type=jnp.float32).astype(jnp.bfloat16)
    value_mix = jnp.dot(rounded, value_low, preferred_element_type=jnp.float32).astype(jnp.bfloat16)
    key_up_grad = jnp.dot(key_mix.T, queries, preferred_element_type=jnp.float32)
    value_up_grad = jnp.dot(value_mix.T, grads, preferred_element_type=jnp.float32)
    return query_gradient, output.astype(jnp.bfloat16), key_up_grad, value_up_grad, key_terms, value_terms


def run_half(queries, grads, keys, values, key_low, value_low, key_up, value_up):
    length = queries.shape[0]
    width = queries.shape[1]
    groups = length // GROUP
    heads_here = width // HEAD_WIDTH

    def grouped_view(array):
        return array.reshape(groups, GROUP, array.shape[1])

    places = jnp.arange(GROUP, dtype=jnp.int32)
    allowed = (places[None, :] <= places[:, None]).astype(jnp.int32)
    grouped = [grouped_view(array) for array in (queries, grads, keys, values)]
    low_keys = grouped_view(key_low)
    low_values = grouped_view(value_low)

    def per_head(head):
        start = head * HEAD_WIDTH

        def column(array):
            return lax.dynamic_slice_in_dim(array, start, HEAD_WIDTH, array.ndim - 1)

        mapped = jax.vmap(head_terms, in_axes=(0, 0, 0, 0, 0, 0, None, None, None))
        return mapped(column(grouped[0]), column(grouped[1]), column(grouped[2]), column(grouped[3]),
                      low_keys, low_values, column(key_up), column(value_up), allowed)

    query_gradient, output, key_up_grad, value_up_grad, key_terms, value_terms = lax.map(
        per_head, jnp.arange(heads_here, dtype=jnp.int32))

    def tokens_first(stacked):
        return jnp.transpose(stacked, (1, 2, 0, 3)).reshape(length, width)

    def rank_first(stacked):
        summed = jnp.sum(stacked, axis=1)
        return jnp.transpose(summed, (1, 0, 2)).reshape(summed.shape[1], width)

    return (tokens_first(query_gradient), tokens_first(output), rank_first(key_up_grad), rank_first(value_up_grad),
            jnp.sum(key_terms, axis=0).reshape(length, ADAPTER_RANK), jnp.sum(value_terms, axis=0).reshape(length, ADAPTER_RANK))


def reference(normed_input, projection_output_gradient, query, key, value, frozen_output_gradient, query_down_weight, query_up_weight, key_down_weight,
              key_up_weight, value_down_weight, value_up_weight, output_down_weight, output_up_weight):
    half_columns = SHIFT_HEADS // 2 * HEAD_WIDTH
    offset = GROUP // 2

    def forward_roll(array):
        return jnp.roll(array, -offset, axis=0)

    def back_roll(array):
        return jnp.roll(array, offset, axis=0)

    def one_sequence(items):
        token_count, incoming_gradient, queries, keys, values, base = items
        reduced_query = jnp.dot(token_count, query_down_weight, preferred_element_type=jnp.float32).astype(jnp.bfloat16)
        reduced_key = jnp.dot(token_count, key_down_weight, preferred_element_type=jnp.float32).astype(jnp.bfloat16)
        reduced_value = jnp.dot(token_count, value_down_weight, preferred_element_type=jnp.float32).astype(jnp.bfloat16)
        reduced_output = jnp.dot(incoming_gradient, output_up_weight.T, preferred_element_type=jnp.float32).astype(jnp.bfloat16)
        grads = (base.astype(jnp.float32)
                 + jnp.dot(reduced_output, output_down_weight.T, preferred_element_type=jnp.float32)).astype(jnp.bfloat16)
        plain = run_half(queries[:, :half_columns], grads[:, :half_columns], keys[:, :half_columns], values[:, :half_columns],
                         reduced_key, reduced_value, key_up_weight[:, :half_columns], value_up_weight[:, :half_columns])
        moved = run_half(forward_roll(queries[:, half_columns:]), forward_roll(grads[:, half_columns:]),
                         forward_roll(keys[:, half_columns:]), forward_roll(values[:, half_columns:]),
                         forward_roll(reduced_key), forward_roll(reduced_value),
                         key_up_weight[:, half_columns:], value_up_weight[:, half_columns:])
        query_gradient = jnp.concatenate([plain[0], back_roll(moved[0])], axis=1)
        attention_probs = jnp.concatenate([plain[1], back_roll(moved[1])], axis=1)
        key_terms = (plain[4] + back_roll(moved[4])).astype(jnp.bfloat16)
        value_terms = (plain[5] + back_roll(moved[5])).astype(jnp.bfloat16)
        reduced_query_gradient = jnp.dot(query_gradient, query_up_weight.T, preferred_element_type=jnp.float32).astype(jnp.bfloat16)
        output_reduced = jnp.dot(attention_probs, output_down_weight, preferred_element_type=jnp.float32).astype(jnp.bfloat16)
        return (jnp.dot(token_count.T, reduced_query_gradient, preferred_element_type=jnp.float32),
                jnp.dot(reduced_query.T, query_gradient, preferred_element_type=jnp.float32),
                jnp.dot(token_count.T, key_terms, preferred_element_type=jnp.float32),
                jnp.concatenate([plain[2], moved[2]], axis=1),
                jnp.dot(token_count.T, value_terms, preferred_element_type=jnp.float32),
                jnp.concatenate([plain[3], moved[3]], axis=1),
                jnp.dot(attention_probs.T, reduced_output, preferred_element_type=jnp.float32),
                jnp.dot(output_reduced.T, incoming_gradient, preferred_element_type=jnp.float32))

    per_sequence = lax.map(one_sequence, (normed_input, projection_output_gradient, query, key, value, frozen_output_gradient))
    return (jnp.sum(per_sequence[0], axis=0), jnp.sum(per_sequence[1], axis=0),
            jnp.sum(per_sequence[2], axis=0), jnp.sum(per_sequence[3], axis=0),
            jnp.sum(per_sequence[4], axis=0), jnp.sum(per_sequence[5], axis=0),
            jnp.sum(per_sequence[6], axis=0), jnp.sum(per_sequence[7], axis=0))
```

```python
import functools
import math

import jax
import jax.numpy as jnp
from jax import lax
from jax.experimental import pallas as pl
from jax.experimental.pallas import tpu as pltpu
from jax.sharding import PartitionSpec as P

SHIFT_HEADS = 16
HEAD_WIDTH = 128
ADAPTER_RANK = 8
GROUP = 2048

HALF_HEADS = SHIFT_HEADS // 2
HALF_COLUMNS = HALF_HEADS * HEAD_WIDTH
SCALE = HEAD_WIDTH ** (-0.5)
LOG2E = math.log2(math.e)
MASKED = -1e30
F32 = jnp.float32
BF16 = jnp.bfloat16
NT = (((1,), (1,)), ((), ()))
BLOCK = 256
VMEM_LIMIT = 56 * 1024 * 1024


def dot(a, b):
    return jnp.dot(a, b, preferred_element_type=F32)


def dot_nt(a, b):
    return lax.dot_general(a, b, NT, preferred_element_type=F32)


def whole():
    return pl.BlockSpec(memory_space=pltpu.VMEM)


def scalars():
    return pl.BlockSpec(memory_space=pltpu.SMEM)


def call(kernel, out_shape, inputs, scratch=(), flops=0, moved=0, exps=0):
    return pl.pallas_call(
        kernel,
        out_shape=out_shape,
        in_specs=[scalars() if i == 0 else whole() for i in range(len(inputs))],
        out_specs=jax.tree.map(lambda _: whole(), out_shape),
        scratch_shapes=list(scratch),
        compiler_params=pltpu.CompilerParams(vmem_limit_bytes=VMEM_LIMIT),
        cost_estimate=pl.CostEstimate(flops=flops, bytes_accessed=moved, transcendentals=exps),
    )(*inputs)


def head_columns(ref, head):
    return ref[:, pl.ds(pl.multiple_of(head * HEAD_WIDTH, HEAD_WIDTH), HEAD_WIDTH)]


def tokens_first(rows):
    pad = jnp.zeros((HEAD_WIDTH - rows.shape[0], rows.shape[1]), F32)
    return jnp.transpose(jnp.concatenate([rows, pad], axis=0))


def pack_kernel(info, x, pog, q, k, v, f, qd, kd, vd, ou, od, out, cross):
    tok = x.shape[0]
    down = jnp.concatenate([qd[...], kd[...], vd[...]], axis=0)
    low = dot_nt(down, x[...])
    low_out = dot_nt(ou[...], pog[...])
    low = jnp.concatenate([low, low_out], axis=0)
    low_b = low.astype(BF16)
    by_token = tokens_first(low_b.astype(F32)).astype(BF16)[:, :32]
    up = jnp.concatenate([jnp.zeros((24, od.shape[1]), BF16), od[...]], axis=0)
    grads = (f[...].astype(F32) + dot(by_token, up)).astype(BF16)
    low_kv = low_b.astype(F32)[8:24].astype(BF16)
    odd = info[0] == 1

    def pick(array, j, first):
        plain = array[:, j * HEAD_WIDTH:(j + 1) * HEAD_WIDTH]
        moved = array[:, HALF_COLUMNS + j * HEAD_WIDTH:HALF_COLUMNS + (j + 1) * HEAD_WIDTH]
        return jnp.where(odd, moved, plain) if first else jnp.where(odd, plain, moved)

    for j in range(HALF_HEADS):
        for i, first in enumerate((True, False)):
            for a, array in enumerate((q, k, v, grads)):
                piece = pick(array, j, first)
                out[j, (4 * i + a) * tok:(4 * i + a + 1) * tok, :] = piece
                if first and a in (1, 2):
                    cross[j, (a - 1) * tok:a * tok, :] = piece
        out[j, 8 * tok:8 * tok + 32, :] = low_b
        cross[j, 2 * tok:2 * tok + 16, :] = low_kv


def attend(head, base, prev, r1, r2, qu, ku, vu, od, kext, vext, sums, emit_terms, emit_head):
    peers = r1.shape[0]
    tok = HEAD_WIDTH
    length = peers * tok
    lead = length if prev else 0
    low = []
    for p in range(peers):
        rows = r1[p, 8 * tok:8 * tok + 32, :]
        low.append(rows)
        t = tokens_first(rows.astype(F32)).astype(BF16)
        at = lead + p * tok
        kext[at:at + tok, :tok] = r1[p, (base + 1) * tok:(base + 2) * tok, :]
        vext[at:at + tok, :tok] = r1[p, (base + 2) * tok:(base + 3) * tok, :]
        kext[at:at + tok, tok:] = t
        vext[at:at + tok, tok:] = t
        if prev:
            at = p * tok
            kext[at:at + tok, :tok] = r2[p, :tok, :]
            vext[at:at + tok, :tok] = r2[p, tok:2 * tok, :]
            rows = r2[p, 2 * tok:2 * tok + 16, :].astype(F32)
            t = tokens_first(jnp.concatenate([jnp.zeros((8, tok), F32), rows], axis=0)).astype(BF16)
            kext[at:at + tok, tok:] = t
            vext[at:at + tok, tok:] = t
    low = jnp.concatenate(low, axis=1).astype(F32)
    low_q = low[0:8].astype(BF16)
    low_o = low[24:32].astype(BF16)
    up_q = head_columns(qu, head)
    up_k = head_columns(ku, head)
    up_v = head_columns(vu, head)
    down = head_columns(od, head)
    total = lead + length
    sums[...] = jnp.zeros_like(sums)
    bq = jnp.zeros((8, HEAD_WIDTH), F32)
    bk, bv, ao = bq, bq, bq
    factor = SCALE * LOG2E
    rows_of = lax.broadcasted_iota(jnp.int32, (BLOCK, BLOCK), 0)
    columns_of = lax.broadcasted_iota(jnp.int32, (BLOCK, BLOCK), 1)
    causal = columns_of <= rows_of
    per = BLOCK // tok
    for b in range(length // BLOCK):
        def block(a):
            return jnp.concatenate(
                [r1[p, (base + a) * tok:(base + a + 1) * tok, :] for p in range(b * per, (b + 1) * per)], axis=0)
        qb, gb = block(0), block(3)
        past = lead + b * BLOCK
        reach = past + BLOCK
        scores = dot_nt(qb, kext[:reach, :tok])
        diagonal = jnp.where(causal, scores[:, past:], MASKED)
        scores = jnp.concatenate([scores[:, :past], diagonal], axis=1) if past else diagonal
        summit = jnp.max(scores, axis=1, keepdims=True)
        e = jnp.exp2((scores - summit) * factor)
        inv = 1.0 / jnp.sum(e, axis=1, keepdims=True)
        p = e.astype(BF16)
        mixed = dot(p, vext[:reach, :])
        output = mixed[:, :tok] * inv
        delta = jnp.sum(gb.astype(F32) * output, axis=1, keepdims=True)
        dweights = dot_nt(gb, vext[:reach, :tok])
        ds = (e * (dweights - delta)).astype(BF16)
        dmixed = dot(ds, kext[:reach, :])
        row_scale = inv * SCALE
        dq = (dmixed[:, :tok] * row_scale).astype(BF16)
        qs = (qb.astype(F32) * row_scale).astype(BF16)
        gs = (gb.astype(F32) * inv).astype(BF16)
        ob = output.astype(BF16)
        sums[0:8, :reach] += dot(dot_nt(up_k, qs).astype(BF16), ds)
        sums[8:16, :reach] += dot(dot_nt(up_v, gs).astype(BF16), p)
        bk += dot(jnp.transpose(dmixed[:, tok:])[8:16].astype(BF16), qs)
        bv += dot(jnp.transpose(mixed[:, tok:])[16:24].astype(BF16), gs)
        bq += dot(low_q[:, b * BLOCK:(b + 1) * BLOCK], dq)
        ao += dot(low_o[:, b * BLOCK:(b + 1) * BLOCK], ob)
        low_dq = dot_nt(up_q, dq)
        out_red = dot_nt(down, ob)
        for i in range(per):
            emit_terms(b * per + i, 0, low_dq[:, i * tok:(i + 1) * tok])
            emit_terms(b * per + i, 8, out_red[:, i * tok:(i + 1) * tok])
    for p in range(peers):
        at = lead + p * tok
        emit_terms(p, 16, sums[:, at:at + tok])
        if prev:
            emit_terms(p, 32, sums[:, p * tok:(p + 1) * tok])
    emit_head(jnp.concatenate([bq, bk, bv, ao], axis=0))


def first_kernel(info, r1, qu, ku, vu, od, terms, head, kext, vext, sums):
    def emit_terms(p, row, value):
        terms[p, row:row + value.shape[0], :] = value

    def emit_head(value):
        head[...] = value

    attend(info[1], 0, False, r1, None, qu, ku, vu, od, kext, vext, sums, emit_terms, emit_head)


def second_kernel(info, r1, r2, qu, ku, vu, od, first_terms, terms, head, kext, vext, sums):
    def emit_terms(p, row, value):
        if row < 32:
            value = value + first_terms[p, row:row + value.shape[0], :]
        terms[p, row:row + value.shape[0], :] = value

    def emit_head(value):
        head[...] = value

    attend(info[2], 4, True, r1, r2, qu, ku, vu, od, kext, vext, sums, emit_terms, emit_head)


def product_kernel(direct, info, terms, back, x, pog, head_f, head_s, *outs):
    own = jnp.sum(terms[:, :32, :], axis=0)
    mixed = own[16:32] + back[...]
    left = jnp.concatenate([own[0:8], mixed], axis=0).astype(BF16)
    right = own[8:16].astype(BF16)
    wide = x.shape[1] // HEAD_WIDTH
    odd = info[0] == 1
    f, s = head_f[...], head_s[...]
    head = jnp.concatenate([jnp.where(odd, s, f), jnp.where(odd, f, s)], axis=0).astype(BF16)
    slot = info[3]
    step = 4
    for c in range(0, wide, step):
        columns = slice(c * HEAD_WIDTH, (c + step) * HEAD_WIDTH)
        a = jnp.concatenate([dot(left, x[:, columns]), dot(right, pog[:, columns])], axis=0).astype(BF16)
        for i in range(step):
            outs[0][c + i, :32, :] = a[:, i * HEAD_WIDTH:(i + 1) * HEAD_WIDTH]
    if direct:
        share = 64 // (wide // HALF_HEADS)
        outs[0][:, 32:, :] = jnp.zeros((wide, share, HEAD_WIDTH), BF16)
        for i in range(wide // HALF_HEADS):
            outs[0][slot * (wide // HALF_HEADS) + i, 32:, :] = head[i * share:(i + 1) * share]
    else:
        outs[1][...] = jnp.zeros(outs[1].shape, BF16)
        outs[1][slot] = head


def share_kernel(info, parts, out):
    summed = jnp.sum(parts[...].astype(F32), axis=0).astype(BF16)
    out[...] = jnp.broadcast_to(summed[None], out.shape)


def finish_kernel(info, main, *refs):
    if len(refs) == 9:
        heads, outs = refs[0], refs[1:]
    else:
        heads, outs = None, refs
    wide = outs[0].shape[1] // HEAD_WIDTH
    per = wide // HALF_HEADS
    for c in range(wide):
        rows = main[c].astype(F32)
        for i, o in enumerate((0, 2, 4, 7)):
            outs[o][:, c * HEAD_WIDTH:(c + 1) * HEAD_WIDTH] = rows[8 * i:8 * i + 8]
    for j in range(HALF_HEADS):
        if heads is None:
            rows = jnp.concatenate([main[j * per + i, 32:, :] for i in range(per)], axis=0).astype(F32)
        else:
            rows = heads[j].astype(F32)
        for half in range(2):
            at = (j + half * HALF_HEADS) * HEAD_WIDTH
            for i, o in enumerate((1, 3, 5, 6)):
                outs[o][:, at:at + HEAD_WIDTH] = rows[32 * half + 8 * i:32 * half + 8 * i + 8]


def per_device(
    devices,
    normed_input,
    projection_output_gradient,
    query,
    key,
    value,
    frozen_output_gradient,
    query_down_weight,
    query_up_weight,
    key_down_weight,
    key_up_weight,
    value_down_weight,
    value_up_weight,
    output_down_weight,
    output_up_weight,
):
    x = normed_input[0]
    pog = projection_output_gradient[0]
    tok, width = x.shape
    peers = GROUP // 2 // tok
    count = lax.axis_size("ctx")
    groups = [list(range(s, s + peers)) for s in range(0, count, peers)]
    my_index = lax.axis_index("ctx")
    odd = (my_index // peers) % 2
    slot = my_index % peers
    info = jnp.stack([odd, slot + HALF_HEADS * odd, slot + HALF_HEADS * (1 - odd), slot]).astype(jnp.int32)
    down_t = output_down_weight.T
    ahead = [(s, (s + peers) % count) for s in range(count)]
    behind = [(t, s) for s, t in ahead]

    def swap(array):
        return lax.all_to_all(array, "ctx", 0, 0, axis_index_groups=groups)

    payload, cross = call(
        pack_kernel,
        (
            jax.ShapeDtypeStruct((peers, 8 * tok + 32, HEAD_WIDTH), BF16),
            jax.ShapeDtypeStruct((peers, 2 * tok + 16, HEAD_WIDTH), BF16),
        ),
        (info, x, pog, query[0], key[0], value[0], frozen_output_gradient[0], query_down_weight.T,
         key_down_weight.T, value_down_weight.T, output_up_weight, down_t),
        flops=2 * 40 * tok * width,
        moved=7 << 20,
    )
    cross = lax.ppermute(cross, "ctx", ahead)
    r1 = swap(payload)
    r2 = swap(cross)
    length = peers * tok
    ups = (query_up_weight, key_up_weight, value_up_weight, down_t)

    def scratch(keys):
        return (
            pltpu.VMEM((keys, 2 * HEAD_WIDTH), BF16),
            pltpu.VMEM((keys, 2 * HEAD_WIDTH), BF16),
            pltpu.VMEM((16, keys), F32),
        )

    pairs = length * length
    first_terms, head_f = call(
        first_kernel,
        (
            jax.ShapeDtypeStruct((peers, 32, HEAD_WIDTH), F32),
            jax.ShapeDtypeStruct((32, HEAD_WIDTH), F32),
        ),
        (info, r1) + ups,
        scratch(length),
        flops=pairs * 6 * 256,
        moved=3 << 20,
        exps=pairs // 2,
    )
    terms, head_s = call(
        second_kernel,
        (
            jax.ShapeDtypeStruct((peers, 48, HEAD_WIDTH), F32),
            jax.ShapeDtypeStruct((32, HEAD_WIDTH), F32),
        ),
        (info, r1, r2) + ups + (first_terms,),
        scratch(2 * length),
        flops=3 * pairs * 6 * 256,
        moved=3 << 20,
        exps=3 * pairs // 2,
    )
    terms = swap(terms)
    back = lax.ppermute(jnp.sum(terms[:, 32:, :], axis=0), "ctx", behind)
    wide = width // HEAD_WIDTH
    share = HALF_HEADS * 64 // devices
    direct = devices == wide and share % 16 == 0
    if direct:
        shapes = (jax.ShapeDtypeStruct((wide, 32 + share, HEAD_WIDTH), BF16),)
    else:
        shapes = (
            jax.ShapeDtypeStruct((wide, 32, HEAD_WIDTH), BF16),
            jax.ShapeDtypeStruct((HALF_HEADS, 64, HEAD_WIDTH), BF16),
        )
    parts = call(
        functools.partial(product_kernel, direct),
        shapes,
        (info, terms, back, x, pog, head_f, head_s),
        flops=2 * 32 * tok * width,
        moved=3 << 20,
    )
    rows = [wide * 32 // devices, share]
    if direct:
        parts = parts[0]
    else:
        parts = jnp.concatenate(
            [part.reshape(devices, n, HEAD_WIDTH) for part, n in zip(parts, rows)], axis=1)
    parts = lax.all_to_all(parts, ("ctx", "dp"), 0, 0)
    shared = call(
        share_kernel,
        jax.ShapeDtypeStruct(parts.shape, BF16),
        (info, parts),
        moved=1 << 20,
    )
    gathered = lax.all_to_all(shared, ("ctx", "dp"), 0, 0)
    if direct:
        gathered = (gathered,)
    else:
        gathered = (
            gathered[:, :rows[0]].reshape(wide, 32, HEAD_WIDTH),
            gathered[:, rows[0]:].reshape(HALF_HEADS, 64, HEAD_WIDTH),
        )
    narrow = SHIFT_HEADS * HEAD_WIDTH
    columns = (width, narrow, width, narrow, width, narrow, narrow, width)
    outs = call(
        finish_kernel,
        tuple(jax.ShapeDtypeStruct((ADAPTER_RANK, n), F32) for n in columns),
        (info,) + gathered,
        moved=2 << 20,
    )
    return tuple(out.T if i in (0, 2, 4, 6) else out for i, out in enumerate(outs))


def solution(mesh):
    placed = (P("dp", "ctx", None),) * 6 + (P(),) * 8
    return jax.shard_map(
        functools.partial(per_device, mesh.size),
        mesh=mesh,
        in_specs=placed,
        out_specs=(P(),) * 8,
        check_vma=False,
    )
```

```python
import functools
import math

import jax
import jax.numpy as jnp
from jax import lax
from jax.experimental import pallas as pl
from jax.experimental.pallas import tpu as pltpu
from jax.sharding import PartitionSpec as P

SHIFT_HEADS = 16
HEAD_WIDTH = 128
ADAPTER_RANK = 8
GROUP = 2048

HALF_HEADS = SHIFT_HEADS // 2
HALF_COLUMNS = HALF_HEADS * HEAD_WIDTH
SCALE = HEAD_WIDTH ** (-0.5)
LOG2E = math.log2(math.e)
MASKED = -1e30
F32 = jnp.float32
BF16 = jnp.bfloat16
NT = (((1,), (1,)), ((), ()))
BLOCK = 256
VMEM_LIMIT = 56 * 1024 * 1024


def dot(a, b):
    return jnp.dot(a, b, preferred_element_type=F32)


def dot_nt(a, b):
    return lax.dot_general(a, b, NT, preferred_element_type=F32)


def whole():
    return pl.BlockSpec(memory_space=pltpu.VMEM)


def scalars():
    return pl.BlockSpec(memory_space=pltpu.SMEM)


def call(kernel, out_shape, inputs, scratch=(), flops=0, moved=0, exps=0):
    return pl.pallas_call(
        kernel,
        out_shape=out_shape,
        in_specs=[scalars() if i == 0 else whole() for i in range(len(inputs))],
        out_specs=jax.tree.map(lambda _: whole(), out_shape),
        scratch_shapes=list(scratch),
        compiler_params=pltpu.CompilerParams(vmem_limit_bytes=VMEM_LIMIT),
        cost_estimate=pl.CostEstimate(flops=flops, bytes_accessed=moved, transcendentals=exps),
    )(*inputs)


def head_columns(ref, head):
    return ref[:, pl.ds(pl.multiple_of(head * HEAD_WIDTH, HEAD_WIDTH), HEAD_WIDTH)]


def tokens_first(rows):
    pad = jnp.zeros((HEAD_WIDTH - rows.shape[0], rows.shape[1]), F32)
    return jnp.transpose(jnp.concatenate([rows, pad], axis=0))


def pack_first_kernel(info, x, pog, q, k, v, f, qd, kd, vd, ou, od, out, grads_low):
    tok = x.shape[0]
    down = jnp.concatenate([qd[...], kd[...], vd[...]], axis=0)
    low = dot_nt(down, x[...])
    low_out = dot_nt(ou[...], pog[...])
    low = jnp.concatenate([low[0:8], low_out, low[8:24]], axis=0)
    low_b = low.astype(BF16)
    by_token = tokens_first(low_b.astype(F32)).astype(BF16)
    grads_low[...] = by_token
    pack_heads(by_token, q, k, v, f, od, out, 2 * tok + 32)
    for j in range(HALF_HEADS):
        out[j, 2 * tok:2 * tok + 32, :] = low_b


def pack_second_kernel(info, by_token, q, k, v, f, od, out):
    pack_heads(by_token[...], q, k, v, f, od, out, 2 * q.shape[0])


def pack_heads(by_token, q, k, v, f, od, out, keys_at):
    tok = q.shape[0]
    width = od.shape[1]
    up = jnp.concatenate([jnp.zeros((8, width), BF16), od[...], jnp.zeros((16, width), BF16)], axis=0)
    grads = (f[...].astype(F32) + dot(by_token[:, :32], up)).astype(BF16)
    for j in range(HALF_HEADS):
        columns = slice(j * HEAD_WIDTH, (j + 1) * HEAD_WIDTH)
        out[j, :tok, :] = q[:, columns]
        out[j, tok:2 * tok, :] = grads[:, columns]
        out[j, keys_at:keys_at + tok, :] = k[:, columns]
        out[j, keys_at + tok:keys_at + 2 * tok, :] = v[:, columns]


def call_on_half(kernel, second, out_shape, info, inputs, halved, moved):
    def spec(i, array):
        if i in halved:
            block = (array.shape[0], HALF_COLUMNS)
            if second:
                return pl.BlockSpec(block, lambda _, s: (0, 1 - s[0]))
            return pl.BlockSpec(block, lambda _, s: (0, s[0]))
        return pl.BlockSpec(array.shape, lambda _, s: (0, 0))

    return pl.pallas_call(
        kernel,
        out_shape=out_shape,
        grid_spec=pltpu.PrefetchScalarGridSpec(
            num_scalar_prefetch=1,
            grid=(1,),
            in_specs=[spec(i, array) for i, array in enumerate(inputs)],
            out_specs=jax.tree.map(
                lambda o: pl.BlockSpec(o.shape, lambda _, s, n=len(o.shape): (0,) * n), out_shape),
        ),
        compiler_params=pltpu.CompilerParams(vmem_limit_bytes=VMEM_LIMIT),
        cost_estimate=pl.CostEstimate(flops=1 << 28, bytes_accessed=moved, transcendentals=0),
    )(info, *inputs)


def attend(head, r1, keys_at, low_rows, cross, qu, ku, vu, od, kext, vext, sums, emit_terms, emit_head):
    prev = cross is not None
    peers = r1.shape[0]
    tok = HEAD_WIDTH
    length = peers * tok
    lead = length if prev else 0
    low = []
    for p in range(peers):
        rows = low_rows(p)
        low.append(rows)
        t = tokens_first(rows.astype(F32)).astype(BF16)
        at = lead + p * tok
        kext[at:at + tok, :tok] = r1[p, keys_at:keys_at + tok, :]
        vext[at:at + tok, :tok] = r1[p, keys_at + tok:keys_at + 2 * tok, :]
        kext[at:at + tok, tok:] = t
        vext[at:at + tok, tok:] = t
        if prev:
            at = p * tok
            kext[at:at + tok, :tok] = cross[p, 16:16 + tok, :]
            vext[at:at + tok, :tok] = cross[p, 16 + tok:16 + 2 * tok, :]
            rows = cross[p, :16, :].astype(F32)
            t = tokens_first(jnp.concatenate([jnp.zeros((16, tok), F32), rows], axis=0)).astype(BF16)
            kext[at:at + tok, tok:] = t
            vext[at:at + tok, tok:] = t
    low = jnp.concatenate(low, axis=1).astype(F32)
    low_q = low[0:8].astype(BF16)
    low_o = low[8:16].astype(BF16)
    up_q = head_columns(qu, head)
    up_k = head_columns(ku, head)
    up_v = head_columns(vu, head)
    down = head_columns(od, head)
    total = lead + length
    sums[...] = jnp.zeros_like(sums)
    bq = jnp.zeros((8, HEAD_WIDTH), F32)
    bk, bv, ao = bq, bq, bq
    factor = SCALE * LOG2E
    rows_of = lax.broadcasted_iota(jnp.int32, (BLOCK, BLOCK), 0)
    columns_of = lax.broadcasted_iota(jnp.int32, (BLOCK, BLOCK), 1)
    causal = columns_of <= rows_of
    per = BLOCK // tok
    for b in range(length // BLOCK):
        def block(a):
            return jnp.concatenate(
                [r1[p, a * tok:(a + 1) * tok, :] for p in range(b * per, (b + 1) * per)], axis=0)
        qb, gb = block(0), block(1)
        past = lead + b * BLOCK
        reach = past + BLOCK
        scores = dot_nt(qb, kext[:reach, :tok])
        diagonal = jnp.where(causal, scores[:, past:], MASKED)
        scores = jnp.concatenate([scores[:, :past], diagonal], axis=1) if past else diagonal
        summit = jnp.max(scores, axis=1, keepdims=True)
        e = jnp.exp2((scores - summit) * factor)
        inv = 1.0 / jnp.sum(e, axis=1, keepdims=True)
        p = e.astype(BF16)
        mixed = dot(p, vext[:reach, :])
        output = mixed[:, :tok] * inv
        delta = jnp.sum(gb.astype(F32) * output, axis=1, keepdims=True)
        dweights = dot_nt(gb, vext[:reach, :tok])
        ds = (e * (dweights - delta)).astype(BF16)
        dmixed = dot(ds, kext[:reach, :])
        row_scale = inv * SCALE
        dq = (dmixed[:, :tok] * row_scale).astype(BF16)
        qs = (qb.astype(F32) * row_scale).astype(BF16)
        gs = (gb.astype(F32) * inv).astype(BF16)
        ob = output.astype(BF16)
        sums[0:8, :reach] += dot(dot_nt(up_k, qs).astype(BF16), ds)
        sums[8:16, :reach] += dot(dot_nt(up_v, gs).astype(BF16), p)
        bk += dot(jnp.transpose(dmixed[:, tok:])[16:24].astype(BF16), qs)
        bv += dot(jnp.transpose(mixed[:, tok:])[24:32].astype(BF16), gs)
        bq += dot(low_q[:, b * BLOCK:(b + 1) * BLOCK], dq)
        ao += dot(low_o[:, b * BLOCK:(b + 1) * BLOCK], ob)
        low_dq = dot_nt(up_q, dq)
        out_red = dot_nt(down, ob)
        for i in range(per):
            emit_terms(b * per + i, 0, low_dq[:, i * tok:(i + 1) * tok])
            emit_terms(b * per + i, 8, out_red[:, i * tok:(i + 1) * tok])
    for p in range(peers):
        at = lead + p * tok
        emit_terms(p, 16, sums[:, at:at + tok])
        if prev:
            emit_terms(p, 32, sums[:, p * tok:(p + 1) * tok])
    emit_head(jnp.concatenate([bq, bk, bv, ao], axis=0))


def first_kernel(info, r1, qu, ku, vu, od, terms, head, low, kext, vext, sums):
    def emit_terms(p, row, value):
        terms[p, row:row + value.shape[0], :] = value

    def emit_head(value):
        head[...] = value

    def low_rows(p):
        rows = r1[p, 2 * HEAD_WIDTH:2 * HEAD_WIDTH + 32, :]
        low[p] = rows
        return rows

    attend(info[1], r1, 2 * HEAD_WIDTH + 32, low_rows, None, qu, ku, vu, od, kext, vext, sums, emit_terms, emit_head)


def second_kernel(near, info, r1, low, cross, qu, ku, vu, od, first_terms, terms, head, kext, vext, sums):
    peers = r1.shape[0]
    if near:
        own = info[0] * peers
        other = peers - own
        for p in range(peers):
            terms[other + p, :16, :] = jnp.zeros((16, HEAD_WIDTH), F32)

    def emit_terms(p, row, value):
        rows = value.shape[0]
        if row < 32:
            value = value + first_terms[p, row:row + rows, :]
        if not near:
            terms[p, row:row + rows, :] = value
        elif row < 32:
            terms[own + p, row:row + rows, :] = value
        else:
            terms[other + p, row - 16:row - 16 + rows, :] = value

    def emit_head(value):
        head[...] = value

    attend(info[2], r1, 2 * HEAD_WIDTH, lambda p: low[p], cross, qu, ku, vu, od, kext, vext, sums, emit_terms, emit_head)


def product_kernel(direct, near, info, terms, *refs):
    own = jnp.sum(terms[:, :32, :], axis=0)
    mixed = own[16:32]
    if not near:
        mixed = mixed + refs[0][...]
        refs = refs[1:]
    x, pog, head_f, head_s, *outs = refs
    left = jnp.concatenate([own[0:8], mixed], axis=0).astype(BF16)
    right = own[8:16].astype(BF16)
    wide = x.shape[1] // HEAD_WIDTH
    odd = info[0] == 1
    f, s = head_f[...], head_s[...]
    head = jnp.concatenate([jnp.where(odd, s, f), jnp.where(odd, f, s)], axis=0).astype(BF16)
    slot = info[3]
    step = 4
    for c in range(0, wide, step):
        columns = slice(c * HEAD_WIDTH, (c + step) * HEAD_WIDTH)
        a = jnp.concatenate([dot(left, x[:, columns]), dot(right, pog[:, columns])], axis=0).astype(BF16)
        for i in range(step):
            outs[0][c + i, :32, :] = a[:, i * HEAD_WIDTH:(i + 1) * HEAD_WIDTH]
    if direct:
        share = 64 // (wide // HALF_HEADS)
        outs[0][:, 32:, :] = jnp.zeros((wide, share, HEAD_WIDTH), BF16)
        for i in range(wide // HALF_HEADS):
            outs[0][slot * (wide // HALF_HEADS) + i, 32:, :] = head[i * share:(i + 1) * share]
    else:
        outs[1][...] = jnp.zeros(outs[1].shape, BF16)
        outs[1][slot] = head


def share_kernel(info, parts, out):
    summed = jnp.sum(parts[...].astype(F32), axis=0).astype(BF16)
    out[...] = jnp.broadcast_to(summed[None], out.shape)


def finish_kernel(kind, info, *refs):
    outs = refs[-8:]
    refs = refs[:-8]
    wide = outs[0].shape[1] // HEAD_WIDTH
    per = wide // HALF_HEADS
    zero = info[4] == 0

    def chunk(c):
        if kind == "paired":
            mine, other = refs[0][c // 2], refs[1][c // 2]
            return jnp.where(zero, mine, other) if c % 2 == 0 else jnp.where(zero, other, mine)
        return refs[0][c]

    head = []
    for c in range(wide):
        rows = chunk(c).astype(F32)
        for i, o in enumerate((0, 2, 4, 7)):
            outs[o][:, c * HEAD_WIDTH:(c + 1) * HEAD_WIDTH] = rows[8 * i:8 * i + 8]
        if kind != "parts":
            head.append(rows[32:])
    for j in range(HALF_HEADS):
        if kind == "parts":
            rows = refs[1][j].astype(F32)
        else:
            rows = jnp.concatenate(head[j * per:(j + 1) * per], axis=0)
        for half in range(2):
            at = (j + half * HALF_HEADS) * HEAD_WIDTH
            for i, o in enumerate((1, 3, 5, 6)):
                outs[o][:, at:at + HEAD_WIDTH] = rows[32 * half + 8 * i:32 * half + 8 * i + 8]


def per_device(
    devices,
    normed_input,
    projection_output_gradient,
    query,
    key,
    value,
    frozen_output_gradient,
    query_down_weight,
    query_up_weight,
    key_down_weight,
    key_up_weight,
    value_down_weight,
    value_up_weight,
    output_down_weight,
    output_up_weight,
):
    x = normed_input[0]
    pog = projection_output_gradient[0]
    tok, width = x.shape
    peers = GROUP // 2 // tok
    count = lax.axis_size("ctx")
    groups = [list(range(s, s + peers)) for s in range(0, count, peers)]
    my_index = lax.axis_index("ctx")
    odd = (my_index // peers) % 2
    slot = my_index % peers
    info = jnp.stack(
        [odd, slot + HALF_HEADS * odd, slot + HALF_HEADS * (1 - odd), slot, lax.axis_index("dp")]).astype(jnp.int32)
    down_t = output_down_weight.T
    ahead = [(s, (s + peers) % count) for s in range(count)]
    behind = [(t, s) for s, t in ahead]
    near = count == 2 * peers

    def swap(array):
        return lax.all_to_all(array, "ctx", 0, 0, axis_index_groups=groups)

    by_head = (query[0], key[0], value[0], frozen_output_gradient[0])
    payload, by_token = call_on_half(
        pack_first_kernel,
        False,
        (
            jax.ShapeDtypeStruct((peers, 4 * tok + 32, HEAD_WIDTH), BF16),
            jax.ShapeDtypeStruct((tok, HEAD_WIDTH), BF16),
        ),
        info,
        (x, pog) + by_head
        + (query_down_weight.T, key_down_weight.T, value_down_weight.T, output_up_weight, down_t),
        (2, 3, 4, 5, 10),
        5 << 20,
    )
    second = call_on_half(
        pack_second_kernel,
        True,
        jax.ShapeDtypeStruct((peers, 4 * tok, HEAD_WIDTH), BF16),
        info,
        (by_token,) + by_head + (down_t,),
        (1, 2, 3, 4, 5),
        2 << 20,
    )
    r1 = swap(payload)
    cross = lax.ppermute(r1[:, 2 * tok + 16:, :], "ctx", ahead)
    r2 = swap(second)
    length = peers * tok
    ups = (query_up_weight, key_up_weight, value_up_weight, down_t)

    def scratch(keys):
        return (
            pltpu.VMEM((keys, 2 * HEAD_WIDTH), BF16),
            pltpu.VMEM((keys, 2 * HEAD_WIDTH), BF16),
            pltpu.VMEM((16, keys), F32),
        )

    pairs = length * length
    first_terms, head_f, low = call(
        first_kernel,
        (
            jax.ShapeDtypeStruct((peers, 32, HEAD_WIDTH), F32),
            jax.ShapeDtypeStruct((32, HEAD_WIDTH), F32),
            jax.ShapeDtypeStruct((peers, 32, HEAD_WIDTH), BF16),
        ),
        (info, r1) + ups,
        scratch(length),
        flops=pairs * 6 * 256,
        moved=3 << 20,
        exps=pairs // 2,
    )
    terms, head_s = call(
        functools.partial(second_kernel, near),
        (
            jax.ShapeDtypeStruct((count, 32, HEAD_WIDTH) if near else (peers, 48, HEAD_WIDTH), F32),
            jax.ShapeDtypeStruct((32, HEAD_WIDTH), F32),
        ),
        (info, r2, low, cross) + ups + (first_terms,),
        scratch(2 * length),
        flops=3 * pairs * 6 * 256,
        moved=3 << 20,
        exps=3 * pairs // 2,
    )
    if near:
        back = ()
        terms = lax.all_to_all(terms, "ctx", 0, 0)
    else:
        terms = swap(terms)
        back = (lax.ppermute(jnp.sum(terms[:, 32:, :], axis=0), "ctx", behind),)
    wide = width // HEAD_WIDTH
    share = HALF_HEADS * 64 // devices
    direct = devices == wide and share % 16 == 0
    if direct:
        shapes = (jax.ShapeDtypeStruct((wide, 32 + share, HEAD_WIDTH), BF16),)
    else:
        shapes = (
            jax.ShapeDtypeStruct((wide, 32, HEAD_WIDTH), BF16),
            jax.ShapeDtypeStruct((HALF_HEADS, 64, HEAD_WIDTH), BF16),
        )
    parts = call(
        functools.partial(product_kernel, direct, near),
        shapes,
        (info, terms) + back + (x, pog, head_f, head_s),
        flops=2 * 32 * tok * width,
        moved=3 << 20,
    )
    rows = [wide * 32 // devices, share]
    if direct:
        parts = parts[0]
    else:
        parts = jnp.concatenate(
            [part.reshape(devices, n, HEAD_WIDTH) for part, n in zip(parts, rows)], axis=1)
    parts = lax.all_to_all(parts, ("ctx", "dp"), 0, 0)
    paired = direct and lax.axis_size("dp") == 2
    shared = call(
        share_kernel,
        jax.ShapeDtypeStruct((count if paired else devices,) + parts.shape[1:], BF16),
        (info, parts),
        moved=1 << 20,
    )
    if paired:
        mine = lax.all_to_all(shared, "ctx", 0, 0)
        gathered = (mine, lax.ppermute(mine, "dp", [(0, 1), (1, 0)]))
    else:
        gathered = (lax.all_to_all(shared, ("ctx", "dp"), 0, 0),)
    if not direct:
        gathered = (
            gathered[0][:, :rows[0]].reshape(wide, 32, HEAD_WIDTH),
            gathered[0][:, rows[0]:].reshape(HALF_HEADS, 64, HEAD_WIDTH),
        )
    kind = "paired" if paired else "whole" if direct else "parts"
    narrow = SHIFT_HEADS * HEAD_WIDTH
    columns = (width, narrow, width, narrow, width, narrow, narrow, width)
    outs = call(
        functools.partial(finish_kernel, kind),
        tuple(jax.ShapeDtypeStruct((ADAPTER_RANK, n), F32) for n in columns),
        (info,) + gathered,
        moved=2 << 20,
    )
    return tuple(out.T if i in (0, 2, 4, 6) else out for i, out in enumerate(outs))


def solution(mesh):
    placed = (P("dp", "ctx", None),) * 6 + (P(),) * 8
    return jax.shard_map(
        functools.partial(per_device, mesh.size),
        mesh=mesh,
        in_specs=placed,
        out_specs=(P(),) * 8,
        check_vma=False,
    )
```

```python
import functools
import math

import jax
import jax.numpy as jnp
from jax import lax
from jax.experimental import pallas as pl
from jax.experimental.pallas import tpu as pltpu
from jax.sharding import PartitionSpec as P

SHIFT_HEADS = 16
HEAD_WIDTH = 128
ADAPTER_RANK = 8
GROUP = 2048

HALF_HEADS = SHIFT_HEADS // 2
HALF_COLUMNS = HALF_HEADS * HEAD_WIDTH
SCALE = HEAD_WIDTH ** (-0.5)
LOG2E = math.log2(math.e)
MASKED = -1e30
F32 = jnp.float32
BF16 = jnp.bfloat16
NT = (((1,), (1,)), ((), ()))
BLOCK = 256
VMEM_LIMIT = 24 * 1024 * 1024
VMEM_WHOLE = 56 * 1024 * 1024


def dot(a, b):
    return jnp.dot(a, b, preferred_element_type=F32)


def dot_nt(a, b):
    return lax.dot_general(a, b, NT, preferred_element_type=F32)


def whole():
    return pl.BlockSpec(memory_space=pltpu.VMEM)


def scalars():
    return pl.BlockSpec(memory_space=pltpu.SMEM)


def call(kernel, out_shape, inputs, scratch=(), flops=0, moved=0, exps=0):
    return pl.pallas_call(
        kernel,
        out_shape=out_shape,
        in_specs=[scalars() if i == 0 else whole() for i in range(len(inputs))],
        out_specs=jax.tree.map(lambda _: whole(), out_shape),
        scratch_shapes=list(scratch),
        compiler_params=pltpu.CompilerParams(vmem_limit_bytes=VMEM_LIMIT),
        cost_estimate=pl.CostEstimate(flops=flops, bytes_accessed=moved, transcendentals=exps),
    )(*inputs)


def head_columns(ref, head):
    return ref[:, pl.ds(pl.multiple_of(head * HEAD_WIDTH, HEAD_WIDTH), HEAD_WIDTH)]


def tokens_first(rows):
    pad = jnp.zeros((HEAD_WIDTH - rows.shape[0], rows.shape[1]), F32)
    return jnp.transpose(jnp.concatenate([rows, pad], axis=0))


def pack_first_kernel(info, x, pog, q, k, v, f, qd, kd, vd, ou, od, out, grads_low):
    tok = x.shape[0]
    down = jnp.concatenate([qd[...], kd[...], vd[...]], axis=0)
    low = dot_nt(down, x[...])
    low_out = dot_nt(ou[...], pog[...])
    low = jnp.concatenate([low[0:8], low_out, low[8:24]], axis=0)
    low_b = low.astype(BF16)
    by_token = tokens_first(low_b.astype(F32)).astype(BF16)
    grads_low[...] = by_token
    grads = all_grads(by_token, f, od)
    for j in range(HALF_HEADS):
        columns = slice(j * HEAD_WIDTH, (j + 1) * HEAD_WIDTH)
        out[j, :tok, :] = q[:, columns]
        out[j, tok:2 * tok, :] = grads[:, columns]
        out[j, 2 * tok:2 * tok + 32, :] = low_b
        out[j, 2 * tok + 32:3 * tok + 32, :] = k[:, columns]
        out[j, 3 * tok + 32:4 * tok + 32, :] = v[:, columns]


def pack_second_kernel(info, by_token, q, k, v, f, od, *outs):
    *outs, grads = outs
    tok = q.shape[0]
    grads[...] = all_grads(by_token[...], f, od)
    for d, out in enumerate(outs):
        peer = jnp.bitwise_xor(info[3], d)
        for i, array in enumerate((q, grads, k, v)):
            out[i * tok:(i + 1) * tok, :] = head_columns(array, peer)


def all_grads(by_token, f, od):
    width = od.shape[1]
    up = jnp.concatenate([jnp.zeros((8, width), BF16), od[...], jnp.zeros((16, width), BF16)], axis=0)
    return (f[...].astype(F32) + dot(by_token[:, :32], up)).astype(BF16)


def call_on_half(kernel, second, out_shape, info, inputs, halved, moved, scratch=()):
    def spec(i, array):
        if i in halved:
            block = (array.shape[0], HALF_COLUMNS)
            if second:
                return pl.BlockSpec(block, lambda _, s: (0, 1 - s[0]))
            return pl.BlockSpec(block, lambda _, s: (0, s[0]))
        return pl.BlockSpec(array.shape, lambda _, s: (0, 0))

    return pl.pallas_call(
        kernel,
        out_shape=out_shape,
        grid_spec=pltpu.PrefetchScalarGridSpec(
            num_scalar_prefetch=1,
            grid=(1,),
            in_specs=[spec(i, array) for i, array in enumerate(inputs)],
            out_specs=jax.tree.map(
                lambda o: pl.BlockSpec(o.shape, lambda _, s, n=len(o.shape): (0,) * n), out_shape),
            scratch_shapes=list(scratch),
        ),
        compiler_params=pltpu.CompilerParams(vmem_limit_bytes=VMEM_LIMIT if second else VMEM_WHOLE),
        cost_estimate=pl.CostEstimate(flops=1 << 28, bytes_accessed=moved, transcendentals=0),
    )(info, *inputs)


def attend(head, low_rows, cross, qu, ku, vu, od, queries, grads, kext, vext, sums, emit):
    prev = cross is not None
    tok = HEAD_WIDTH
    length = queries.shape[0]
    peers = length // tok
    lead = length if prev else 0
    low = []
    for p in range(peers):
        rows = low_rows(p)
        low.append(rows)
        t = tokens_first(rows.astype(F32)).astype(BF16)
        at = lead + p * tok
        kext[at:at + tok, tok:] = t
        vext[at:at + tok, tok:] = t
        if prev:
            at = p * tok
            kext[at:at + tok, :tok] = cross[p, 16:16 + tok, :]
            vext[at:at + tok, :tok] = cross[p, 16 + tok:16 + 2 * tok, :]
            rows = cross[p, :16, :].astype(F32)
            t = tokens_first(jnp.concatenate([jnp.zeros((16, tok), F32), rows], axis=0)).astype(BF16)
            kext[at:at + tok, tok:] = t
            vext[at:at + tok, tok:] = t
    low = jnp.concatenate(low, axis=1).astype(F32)
    low_q = low[0:8].astype(BF16)
    low_o = low[8:16].astype(BF16)
    up_q = head_columns(qu, head)
    up_k = head_columns(ku, head)
    up_v = head_columns(vu, head)
    down = head_columns(od, head)
    total = lead + length
    sums[...] = jnp.zeros_like(sums)
    bq = jnp.zeros((8, HEAD_WIDTH), F32)
    bk, bv, ao = bq, bq, bq
    factor = SCALE * LOG2E
    rows_of = lax.broadcasted_iota(jnp.int32, (BLOCK, BLOCK), 0)
    columns_of = lax.broadcasted_iota(jnp.int32, (BLOCK, BLOCK), 1)
    causal = columns_of <= rows_of
    per = BLOCK // tok
    pairs = []
    for b in range(length // BLOCK):
        qb = queries[b * BLOCK:(b + 1) * BLOCK, :]
        gb = grads[b * BLOCK:(b + 1) * BLOCK, :]
        past = lead + b * BLOCK
        reach = past + BLOCK
        scores = dot_nt(qb, kext[:reach, :tok])
        diagonal = jnp.where(causal, scores[:, past:], MASKED)
        scores = jnp.concatenate([scores[:, :past], diagonal], axis=1) if past else diagonal
        summit = jnp.max(scores, axis=1, keepdims=True)
        e = jnp.exp2((scores - summit) * factor)
        inv = 1.0 / jnp.sum(e, axis=1, keepdims=True)
        p = e.astype(BF16)
        mixed = dot(p, vext[:reach, :])
        output = mixed[:, :tok] * inv
        delta = jnp.sum(gb.astype(F32) * output, axis=1, keepdims=True)
        dweights = dot_nt(gb, vext[:reach, :tok])
        ds = (e * (dweights - delta)).astype(BF16)
        dmixed = dot(ds, kext[:reach, :])
        row_scale = inv * SCALE
        dq = (dmixed[:, :tok] * row_scale).astype(BF16)
        qs = (qb.astype(F32) * row_scale).astype(BF16)
        gs = (gb.astype(F32) * inv).astype(BF16)
        ob = output.astype(BF16)
        sums[0:8, :reach] += dot(dot_nt(up_k, qs).astype(BF16), ds)
        sums[8:16, :reach] += dot(dot_nt(up_v, gs).astype(BF16), p)
        bk += dot(jnp.transpose(dmixed[:, tok:])[16:24].astype(BF16), qs)
        bv += dot(jnp.transpose(mixed[:, tok:])[24:32].astype(BF16), gs)
        bq += dot(low_q[:, b * BLOCK:(b + 1) * BLOCK], dq)
        ao += dot(low_o[:, b * BLOCK:(b + 1) * BLOCK], ob)
        low_dq = dot_nt(up_q, dq)
        out_red = dot_nt(down, ob)
        pair = jnp.concatenate([low_dq, out_red], axis=0)
        pairs += [pair[:, i * tok:(i + 1) * tok] for i in range(per)]
    for p in range(peers):
        at = lead + p * tok
        own = jnp.concatenate([pairs[p], sums[:, at:at + tok]], axis=0)
        emit(p, own, sums[:, p * tok:(p + 1) * tok] if prev else None)
    return jnp.concatenate([bq, bk, bv, ao], axis=0)


def first_kernel(info, r1, qu, ku, vu, od, terms, head, low, queries, grads, kext, vext, sums):
    tok = HEAD_WIDTH
    for p in range(r1.shape[0]):
        at = slice(p * tok, (p + 1) * tok)
        queries[at, :] = r1[p, :tok, :]
        grads[at, :] = r1[p, tok:2 * tok, :]
        low[p] = r1[p, 2 * tok:2 * tok + 32, :]
        kext[at, :tok] = r1[p, 2 * tok + 32:3 * tok + 32, :]
        vext[at, :tok] = r1[p, 3 * tok + 32:4 * tok + 32, :]

    def emit(p, own, previous):
        terms[p] = own

    head[...] = attend(info[1], lambda p: r1[p, 2 * tok:2 * tok + 32, :], None, qu, ku, vu, od,
                       queries, grads, kext, vext, sums, emit)


def second_kernel(near, info, *refs):
    peers = HALF_HEADS
    parts, refs = refs[:peers], refs[peers:]
    low, cross, qu, ku, vu, od, first_terms, terms, head, queries, grads, kext, vext, sums = refs
    tok = HEAD_WIDTH
    length = peers * tok
    for d, part in enumerate(parts):
        at = pl.multiple_of(jnp.bitwise_xor(info[3], d) * tok, tok)
        queries[pl.ds(at, tok), :] = part[:tok, :]
        grads[pl.ds(at, tok), :] = part[tok:2 * tok, :]
        kext[pl.ds(length + at, tok), :tok] = part[2 * tok:3 * tok, :]
        vext[pl.ds(length + at, tok), :tok] = part[3 * tok:, :]
    mine = info[0] * peers
    other = peers - mine

    def emit(p, own, previous):
        own = own + first_terms[p]
        if near:
            terms[mine + p] = own.astype(BF16)
            terms[other + p] = jnp.concatenate([jnp.zeros((16, tok), F32), previous], axis=0).astype(BF16)
        else:
            terms[p] = jnp.concatenate([own, previous], axis=0).astype(BF16)

    head[...] = attend(info[2], lambda p: low[p], cross, qu, ku, vu, od, queries, grads, kext, vext, sums, emit)


def product_kernel(direct, near, info, terms, *refs):
    own = jnp.sum(terms[:, :32, :].astype(F32), axis=0)
    mixed = own[16:32]
    if not near:
        mixed = mixed + refs[0][...]
        refs = refs[1:]
    x, pog, head_f, head_s, *outs = refs
    left = jnp.concatenate([own[0:8], mixed], axis=0).astype(BF16)
    right = own[8:16].astype(BF16)
    wide = x.shape[1] // HEAD_WIDTH
    odd = info[0] == 1
    f, s = head_f[...], head_s[...]
    head = jnp.concatenate([jnp.where(odd, s, f), jnp.where(odd, f, s)], axis=0).astype(BF16)
    slot = info[3]
    step = 4
    for c in range(0, wide, step):
        columns = slice(c * HEAD_WIDTH, (c + step) * HEAD_WIDTH)
        a = jnp.concatenate([dot(left, x[:, columns]), dot(right, pog[:, columns])], axis=0).astype(BF16)
        for i in range(step):
            outs[0][c + i, :32, :] = a[:, i * HEAD_WIDTH:(i + 1) * HEAD_WIDTH]
    if direct:
        share = 64 // (wide // HALF_HEADS)
        outs[0][:, 32:, :] = jnp.zeros((wide, share, HEAD_WIDTH), BF16)
        for i in range(wide // HALF_HEADS):
            outs[0][slot * (wide // HALF_HEADS) + i, 32:, :] = head[i * share:(i + 1) * share]
    else:
        outs[1][...] = jnp.zeros(outs[1].shape, BF16)
        outs[1][slot] = head


def share_kernel(info, parts, out):
    summed = jnp.sum(parts[...].astype(F32), axis=0).astype(BF16)
    out[...] = jnp.broadcast_to(summed[None], out.shape)


def finish_kernel(kind, info, *refs):
    outs = refs[-8:]
    refs = refs[:-8]
    wide = outs[0].shape[1] // HEAD_WIDTH
    per = wide // HALF_HEADS
    zero = info[4] == 0

    def chunk(c):
        if kind == "paired":
            mine, other = refs[0][c // 2], refs[1][c // 2]
            return jnp.where(zero, mine, other) if c % 2 == 0 else jnp.where(zero, other, mine)
        return refs[0][c]

    head = []
    for c in range(wide):
        rows = chunk(c).astype(F32)
        for i, o in enumerate((0, 2, 4, 7)):
            outs[o][:, c * HEAD_WIDTH:(c + 1) * HEAD_WIDTH] = rows[8 * i:8 * i + 8]
        if kind != "parts":
            head.append(rows[32:])
    for j in range(HALF_HEADS):
        if kind == "parts":
            rows = refs[1][j].astype(F32)
        else:
            rows = jnp.concatenate(head[j * per:(j + 1) * per], axis=0)
        for half in range(2):
            at = (j + half * HALF_HEADS) * HEAD_WIDTH
            for i, o in enumerate((1, 3, 5, 6)):
                outs[o][:, at:at + HEAD_WIDTH] = rows[32 * half + 8 * i:32 * half + 8 * i + 8]


def per_device(
    devices,
    normed_input,
    projection_output_gradient,
    query,
    key,
    value,
    frozen_output_gradient,
    query_down_weight,
    query_up_weight,
    key_down_weight,
    key_up_weight,
    value_down_weight,
    value_up_weight,
    output_down_weight,
    output_up_weight,
):
    x = normed_input[0]
    pog = projection_output_gradient[0]
    tok, width = x.shape
    peers = GROUP // 2 // tok
    count = lax.axis_size("ctx")
    groups = [list(range(s, s + peers)) for s in range(0, count, peers)]
    my_index = lax.axis_index("ctx")
    odd = (my_index // peers) % 2
    slot = my_index % peers
    info = jnp.stack(
        [odd, slot + HALF_HEADS * odd, slot + HALF_HEADS * (1 - odd), slot, lax.axis_index("dp")]).astype(jnp.int32)
    down_t = output_down_weight.T
    ahead = [(s, (s + peers) % count) for s in range(count)]
    behind = [(t, s) for s, t in ahead]
    near = count == 2 * peers

    def swap(array):
        return lax.all_to_all(array, "ctx", 0, 0, axis_index_groups=groups)

    by_head = (query[0], key[0], value[0], frozen_output_gradient[0])
    payload, by_token = call_on_half(
        pack_first_kernel,
        False,
        (
            jax.ShapeDtypeStruct((peers, 4 * tok + 32, HEAD_WIDTH), BF16),
            jax.ShapeDtypeStruct((tok, HEAD_WIDTH), BF16),
        ),
        info,
        (x, pog) + by_head
        + (query_down_weight.T, key_down_weight.T, value_down_weight.T, output_up_weight, down_t),
        (2, 3, 4, 5, 10),
        5 << 20,
    )
    second = call_on_half(
        pack_second_kernel,
        True,
        (jax.ShapeDtypeStruct((4 * tok, HEAD_WIDTH), BF16),) * peers,
        info,
        (by_token,) + by_head + (down_t,),
        (1, 2, 3, 4, 5),
        2 << 20,
        (pltpu.VMEM((tok, HALF_COLUMNS), BF16),),
    )
    r1 = swap(payload)
    cross = lax.ppermute(r1[:, 2 * tok + 16:, :], "ctx", ahead)
    r2 = second[:1] + tuple(
        lax.ppermute(second[d], "ctx", [(s, s ^ d) for s in range(count)]) for d in range(1, peers))
    length = peers * tok
    ups = (query_up_weight, key_up_weight, value_up_weight, down_t)

    def scratch(keys):
        return (
            pltpu.VMEM((length, HEAD_WIDTH), BF16),
            pltpu.VMEM((length, HEAD_WIDTH), BF16),
            pltpu.VMEM((keys, 2 * HEAD_WIDTH), BF16),
            pltpu.VMEM((keys, 2 * HEAD_WIDTH), BF16),
            pltpu.VMEM((16, keys), F32),
        )

    pairs = length * length
    first_terms, head_f, low = call(
        first_kernel,
        (
            jax.ShapeDtypeStruct((peers, 32, HEAD_WIDTH), F32),
            jax.ShapeDtypeStruct((32, HEAD_WIDTH), F32),
            jax.ShapeDtypeStruct((peers, 32, HEAD_WIDTH), BF16),
        ),
        (info, r1) + ups,
        scratch(length),
        flops=pairs * 6 * 256,
        moved=3 << 20,
        exps=pairs // 2,
    )
    terms, head_s = call(
        functools.partial(second_kernel, near),
        (
            jax.ShapeDtypeStruct((count, 32, HEAD_WIDTH) if near else (peers, 48, HEAD_WIDTH), BF16),
            jax.ShapeDtypeStruct((32, HEAD_WIDTH), F32),
        ),
        (info,) + r2 + (low, cross) + ups + (first_terms,),
        scratch(2 * length),
        flops=3 * pairs * 6 * 256,
        moved=3 << 20,
        exps=3 * pairs // 2,
    )
    if near:
        back = ()
        terms = lax.all_to_all(terms, "ctx", 0, 0)
    else:
        terms = swap(terms)
        back = (lax.ppermute(jnp.sum(terms[:, 32:, :].astype(F32), axis=0), "ctx", behind),)
    wide = width // HEAD_WIDTH
    share = HALF_HEADS * 64 // devices
    direct = devices == wide and share % 16 == 0
    if direct:
        shapes = (jax.ShapeDtypeStruct((wide, 32 + share, HEAD_WIDTH), BF16),)
    else:
        shapes = (
            jax.ShapeDtypeStruct((wide, 32, HEAD_WIDTH), BF16),
            jax.ShapeDtypeStruct((HALF_HEADS, 64, HEAD_WIDTH), BF16),
        )
    parts = call(
        functools.partial(product_kernel, direct, near),
        shapes,
        (info, terms) + back + (x, pog, head_f, head_s),
        flops=2 * 32 * tok * width,
        moved=3 << 20,
    )
    rows = [wide * 32 // devices, share]
    if direct:
        parts = parts[0]
    else:
        parts = jnp.concatenate(
            [part.reshape(devices, n, HEAD_WIDTH) for part, n in zip(parts, rows)], axis=1)
    parts = lax.all_to_all(parts, ("ctx", "dp"), 0, 0)
    paired = direct and lax.axis_size("dp") == 2
    shared = call(
        share_kernel,
        jax.ShapeDtypeStruct((count if paired else devices,) + parts.shape[1:], BF16),
        (info, parts),
        moved=1 << 20,
    )
    if paired:
        mine = lax.all_to_all(shared, "ctx", 0, 0)
        gathered = (mine, lax.ppermute(mine, "dp", [(0, 1), (1, 0)]))
    else:
        gathered = (lax.all_to_all(shared, ("ctx", "dp"), 0, 0),)
    if not direct:
        gathered = (
            gathered[0][:, :rows[0]].reshape(wide, 32, HEAD_WIDTH),
            gathered[0][:, rows[0]:].reshape(HALF_HEADS, 64, HEAD_WIDTH),
        )
    kind = "paired" if paired else "whole" if direct else "parts"
    narrow = SHIFT_HEADS * HEAD_WIDTH
    columns = (width, narrow, width, narrow, width, narrow, narrow, width)
    outs = call(
        functools.partial(finish_kernel, kind),
        tuple(jax.ShapeDtypeStruct((ADAPTER_RANK, n), F32) for n in columns),
        (info,) + gathered,
        moved=2 << 20,
    )
    return tuple(out.T if i in (0, 2, 4, 6) else out for i, out in enumerate(outs))


def solution(mesh):
    placed = (P("dp", "ctx", None),) * 6 + (P(),) * 8
    return jax.shard_map(
        functools.partial(per_device, mesh.size),
        mesh=mesh,
        in_specs=placed,
        out_specs=(P(),) * 8,
        check_vma=False,
    )
```

```python
import functools
import math

import jax
import jax.numpy as jnp
from jax import lax
from jax.experimental import pallas as pl
from jax.experimental.pallas import tpu as pltpu
from jax.sharding import PartitionSpec as P

SHIFT_HEADS = 16
HEAD_WIDTH = 128
ADAPTER_RANK = 8
GROUP = 2048

HALF_HEADS = SHIFT_HEADS // 2
HALF_COLUMNS = HALF_HEADS * HEAD_WIDTH
SCALE = HEAD_WIDTH ** (-0.5)
LOG2E = math.log2(math.e)
MASKED = -1e30
F32 = jnp.float32
BF16 = jnp.bfloat16
NT = (((1,), (1,)), ((), ()))
ORDERS = ((0, 1, 2, 4, 3, 5, 6, 7), (0, 2, 4, 1, 6, 3, 5, 7))
BLOCK = 256
VMEM_LIMIT = 24 * 1024 * 1024
VMEM_PACK = 56 * 1024 * 1024


def dot(a, b):
    return jnp.dot(a, b, preferred_element_type=F32)


def dot_nt(a, b):
    return lax.dot_general(a, b, NT, preferred_element_type=F32)


def call(kernel, out_shape, inputs, scratch=(), flops=0, moved=0, exps=0, limit=VMEM_LIMIT, far=0):
    return pl.pallas_call(
        kernel,
        out_shape=out_shape,
        in_specs=[pl.BlockSpec(memory_space=pltpu.HBM if i < far else pltpu.VMEM) for i in range(len(inputs))],
        out_specs=jax.tree.map(lambda _: pl.BlockSpec(memory_space=pltpu.VMEM), out_shape),
        scratch_shapes=list(scratch),
        compiler_params=pltpu.CompilerParams(vmem_limit_bytes=limit),
        cost_estimate=pl.CostEstimate(flops=flops, bytes_accessed=moved, transcendentals=exps),
    )(*inputs)


MIRROR = HALF_HEADS // 2


def place():
    index = lax.axis_index("ctx")
    return lax.rem(lax.div(index, HALF_HEADS), 2), lax.rem(index, HALF_HEADS)


def partners():
    _, slot = place()
    core = lax.rem(lax.axis_index("dp"), 2)
    return [jnp.bitwise_xor(slot, jnp.where(core == 0, a, b)) for a, b in zip(*ORDERS)]


def rows_at(index):
    return pl.ds(pl.multiple_of(index * HEAD_WIDTH, HEAD_WIDTH), HEAD_WIDTH)


def head_columns(ref, head):
    return ref[:, pl.ds(pl.multiple_of(head * HEAD_WIDTH, HEAD_WIDTH), HEAD_WIDTH)]


def tokens_first(rows):
    pad = jnp.zeros((HEAD_WIDTH - rows.shape[0], rows.shape[1]), F32)
    return jnp.transpose(jnp.concatenate([rows, pad], axis=0))


def pack_kernel(q, k, v, x, pog, f, qd, kd, vd, ou, od, *refs):
    outs, bufs, sems = refs[:-12], refs[-12:-1], refs[-1]
    firsts, seconds = outs[:HALF_HEADS], outs[HALF_HEADS:]
    qs, ks, vs, xs, ps, fs, qds, kds, vds, ous, ods = bufs
    odd, _ = place()
    tok, width = x.shape
    chunks = 4
    step = width // chunks
    sources = (q, k, v, x, pog, f, qd, kd, vd, ou, od)
    whole = {i: pltpu.make_async_copy(sources[i], bufs[i], sems.at[i]) for i in (0, 1, 2, 5, 6, 7, 8, 9, 10)}
    wide = []
    for c in range(chunks):
        columns = pl.ds(c * step, step)
        wide.append([pltpu.make_async_copy(sources[i].at[:, columns], bufs[i].at[:, columns], sems.at[11 + (i - 3) * chunks + c])
                     for i in (3, 4)])
    for i in (6, 7, 8, 9):
        whole[i].start()
    for pair in wide[:2]:
        for copy in pair:
            copy.start()
    for i in (0, 1, 2):
        whole[i].start()
    for pair in wide[2:]:
        for copy in pair:
            copy.start()
    for i in (10, 5):
        whole[i].start()
    for i in (6, 7, 8, 9):
        whole[i].wait()
    down = jnp.concatenate([qds[...], kds[...], vds[...]], axis=0)
    low = jnp.zeros((24, tok), F32)
    low_out = jnp.zeros((8, tok), F32)
    peers = partners()
    spots = ((0, 0, 0), (1, 2 * tok + 32, 2 * tok), (2, 3 * tok + 32, 3 * tok))
    for c in range(chunks):
        columns = slice(c * step, (c + 1) * step)
        wide[c][0].wait()
        low += dot_nt(down[:, columns], xs[:, columns])
        wide[c][1].wait()
        low_out += dot_nt(ous[:, columns], ps[:, columns])
        if c > 0:
            i, at, late = spots[c - 1]
            whole[i].wait()
            spread(bufs[i], odd, peers, firsts, at, seconds, late)
    low_b = jnp.concatenate([low[0:8], low_out, low[8:24]], axis=0).astype(BF16)
    by_token = tokens_first(low_b.astype(F32)).astype(BF16)
    columns = od.shape[1]
    whole[10].wait()
    up = jnp.concatenate([jnp.zeros((8, columns), BF16), ods[...], jnp.zeros((16, columns), BF16)], axis=0)
    raised = dot(by_token[:, :32], up)
    whole[5].wait()
    fs[...] = (fs[...].astype(F32) + raised).astype(BF16)
    spread(fs, odd, peers, firsts, tok, seconds, tok)
    for first in firsts:
        first[2 * tok:2 * tok + 32, :] = low_b


def spread(array, odd, peers, firsts, at, seconds, late):
    tok = array.shape[0]
    for peer, first, second in zip(peers, firsts, seconds):
        first[at:at + tok, :] = head_columns(array, peer + HALF_HEADS * odd)
        second[late:late + tok, :] = head_columns(array, second_head(peer) + HALF_HEADS * (1 - odd))


def second_head(peer):
    return jnp.bitwise_xor(peer, MIRROR)


def assemble_kernel(*refs):
    parts, cross = refs[:-1], refs[-1]
    for peer, part in zip(partners(), parts):
        cross[peer] = part[2 * HEAD_WIDTH + 16:, :]


def attend(head, lead, low, qu, ku, vu, od, queries, grads, kext, vext, sums, emit):
    tok = HEAD_WIDTH
    length = queries.shape[0]
    peers = length // tok
    low = [low[p] for p in range(peers)]
    low = jnp.concatenate(low, axis=1).astype(F32)
    low_q = low[0:8].astype(BF16)
    low_o = low[8:16].astype(BF16)
    up_q = head_columns(qu, head)
    up_k = head_columns(ku, head)
    up_v = head_columns(vu, head)
    down = head_columns(od, head)
    total = lead + length
    sums[...] = jnp.zeros_like(sums)
    bq = jnp.zeros((8, HEAD_WIDTH), F32)
    bk, bv, ao = bq, bq, bq
    factor = SCALE * LOG2E
    rows_of = lax.broadcasted_iota(jnp.int32, (BLOCK, BLOCK), 0)
    columns_of = lax.broadcasted_iota(jnp.int32, (BLOCK, BLOCK), 1)
    causal = columns_of <= rows_of
    per = BLOCK // tok
    pairs = []
    for b in range(length // BLOCK):
        qb = queries[b * BLOCK:(b + 1) * BLOCK, :]
        gb = grads[b * BLOCK:(b + 1) * BLOCK, :]
        past = lead + b * BLOCK
        reach = past + BLOCK
        scores = dot_nt(qb, kext[:reach, :tok])
        diagonal = jnp.where(causal, scores[:, past:], MASKED)
        scores = jnp.concatenate([scores[:, :past], diagonal], axis=1) if past else diagonal
        summit = jnp.max(scores, axis=1, keepdims=True)
        e = jnp.exp2((scores - summit) * factor)
        inv = 1.0 / jnp.sum(e, axis=1, keepdims=True)
        p = e.astype(BF16)
        mixed = dot(p, vext[:reach, :])
        output = mixed[:, :tok] * inv
        delta = jnp.sum(gb.astype(F32) * output, axis=1, keepdims=True)
        dweights = dot_nt(gb, vext[:reach, :tok])
        ds = (e * (dweights - delta)).astype(BF16)
        dmixed = dot(ds, kext[:reach, :])
        row_scale = inv * SCALE
        dq = (dmixed[:, :tok] * row_scale).astype(BF16)
        qs = (qb.astype(F32) * row_scale).astype(BF16)
        gs = (gb.astype(F32) * inv).astype(BF16)
        ob = output.astype(BF16)
        sums[0:8, :reach] += dot(dot_nt(up_k, qs).astype(BF16), ds)
        sums[8:16, :reach] += dot(dot_nt(up_v, gs).astype(BF16), p)
        bk += dot(jnp.transpose(dmixed[:, tok:])[16:24].astype(BF16), qs)
        bv += dot(jnp.transpose(mixed[:, tok:])[24:32].astype(BF16), gs)
        bq += dot(low_q[:, b * BLOCK:(b + 1) * BLOCK], dq)
        ao += dot(low_o[:, b * BLOCK:(b + 1) * BLOCK], ob)
        low_dq = dot_nt(up_q, dq)
        out_red = dot_nt(down, ob)
        pair = jnp.concatenate([low_dq, out_red], axis=0)
        pairs += [pair[:, i * tok:(i + 1) * tok] for i in range(per)]
    for p in range(peers):
        at = lead + p * tok
        own = jnp.concatenate([pairs[p], sums[:, at:at + tok]], axis=0)
        emit(p, own, sums[:, p * tok:(p + 1) * tok] if lead else None)
    return jnp.concatenate([bq, bk, bv, ao], axis=0)


def first_kernel(*refs):
    parts, refs = refs[:HALF_HEADS], refs[HALF_HEADS:]
    qu, ku, vu, od, terms, head, low, token_low, queries, grads, kext, vext, sums = refs
    odd, slot = place()
    tok = HEAD_WIDTH
    for peer, part in zip(partners(), parts):
        at = rows_at(peer)
        queries[at, :] = part[:tok, :]
        grads[at, :] = part[tok:2 * tok, :]
        rows = part[2 * tok:2 * tok + 32, :]
        low[peer] = rows
        t = tokens_first(rows.astype(F32)).astype(BF16)
        token_low[at, :] = t
        kext[at, :tok] = part[2 * tok + 32:3 * tok + 32, :]
        vext[at, :tok] = part[3 * tok + 32:, :]
        kext[at, tok:] = t
        vext[at, tok:] = t

    def emit(p, own, previous):
        terms[p] = own

    head[...] = attend(slot + HALF_HEADS * odd, 0, low, qu, ku, vu, od, queries, grads, kext, vext, sums, emit)


def second_kernel(near, *refs):
    parts, refs = refs[:HALF_HEADS], refs[HALF_HEADS:]
    cross, low, token_low, first_terms, head_f, qu, ku, vu, od, terms, heads, queries, grads, kext, vext, sums = refs
    odd, slot = place()
    tok = HEAD_WIDTH
    length = token_low.shape[0]
    for peer, part in zip(partners(), parts):
        at = rows_at(peer)
        late = rows_at(peer + HALF_HEADS)
        queries[at, :] = part[:tok, :]
        grads[at, :] = part[tok:2 * tok, :]
        kext[late, :tok] = part[2 * tok:3 * tok, :]
        vext[late, :tok] = part[3 * tok:, :]
    kext[length:, tok:] = token_low[...]
    vext[length:, tok:] = token_low[...]
    for p in range(HALF_HEADS):
        at = slice(p * tok, (p + 1) * tok)
        rows = jnp.concatenate([jnp.zeros((16, tok), F32), cross[p, :16, :].astype(F32)], axis=0)
        t = tokens_first(rows).astype(BF16)
        kext[at, :tok] = cross[p, 16:16 + tok, :]
        vext[at, :tok] = cross[p, 16 + tok:, :]
        kext[at, tok:] = t
        vext[at, tok:] = t
    mine = odd * HALF_HEADS
    other = HALF_HEADS - mine

    def emit(p, own, previous):
        own = own + first_terms[p]
        if near:
            terms[mine + p] = own.astype(BF16)
            terms[other + p] = jnp.concatenate([jnp.zeros((16, tok), F32), previous], axis=0).astype(BF16)
        else:
            terms[p] = jnp.concatenate([own, previous], axis=0).astype(BF16)

    head_s = attend(second_head(slot) + HALF_HEADS * (1 - odd), length, low, qu, ku, vu, od, queries, grads, kext, vext, sums, emit)
    heads[:32, :] = head_f[...]
    heads[32:, :] = head_s


def product_kernel(direct, near, terms, *refs):
    own = jnp.sum(terms[:, :32, :].astype(F32), axis=0)
    mixed = own[16:32]
    if not near:
        mixed = mixed + refs[0][...]
        refs = refs[1:]
    x, pog, heads, *outs = refs
    left = jnp.concatenate([own[0:8], mixed], axis=0).astype(BF16)
    right = own[8:16].astype(BF16)
    wide = x.shape[1] // HEAD_WIDTH
    head = heads[...].astype(BF16)
    odd, slot = place()
    step = 4
    for c in range(0, wide, step):
        columns = slice(c * HEAD_WIDTH, (c + step) * HEAD_WIDTH)
        a = jnp.concatenate([dot(left, x[:, columns]), dot(right, pog[:, columns])], axis=0).astype(BF16)
        for i in range(step):
            outs[0][c + i, :32, :] = a[:, i * HEAD_WIDTH:(i + 1) * HEAD_WIDTH]
    spots = ((slot, odd), (second_head(slot), 1 - odd))
    if direct:
        per = wide // HALF_HEADS
        share = 64 // per
        outs[0][:, 32:, :] = jnp.zeros((wide, share, HEAD_WIDTH), BF16)
        for i in range(per):
            where, half = spots[2 * i // per]
            outs[0][where * per + half * (per // 2) + i % (per // 2), 32:, :] = head[i * share:(i + 1) * share]
    else:
        outs[1][...] = jnp.zeros(outs[1].shape, BF16)
        for i, (where, half) in enumerate(spots):
            outs[1][where, pl.ds(pl.multiple_of(32 * half, 32), 32), :] = head[32 * i:32 * i + 32]


def share_kernel(parts, out):
    summed = jnp.sum(parts[...].astype(F32), axis=0).astype(BF16)
    out[...] = jnp.broadcast_to(summed[None], out.shape)


def finish_kernel(kind, *refs):
    outs = refs[-8:]
    refs = refs[:-8]
    wide = outs[0].shape[1] // HEAD_WIDTH
    per = wide // HALF_HEADS
    zero = lax.axis_index("dp") == 0

    def chunk(c):
        if kind == "paired":
            mine, other = refs[0][c // 2], refs[1][c // 2]
            return jnp.where(zero, mine, other) if c % 2 == 0 else jnp.where(zero, other, mine)
        return refs[0][c]

    head = []
    for c in range(wide):
        rows = chunk(c).astype(F32)
        for i, o in enumerate((0, 2, 4, 7)):
            outs[o][:, c * HEAD_WIDTH:(c + 1) * HEAD_WIDTH] = rows[8 * i:8 * i + 8]
        if kind != "parts":
            head.append(rows[32:])
    for j in range(HALF_HEADS):
        if kind == "parts":
            rows = refs[1][j].astype(F32)
        else:
            rows = jnp.concatenate(head[j * per:(j + 1) * per], axis=0)
        for half in range(2):
            at = (j + half * HALF_HEADS) * HEAD_WIDTH
            for i, o in enumerate((1, 3, 5, 6)):
                outs[o][:, at:at + HEAD_WIDTH] = rows[32 * half + 8 * i:32 * half + 8 * i + 8]


def per_device(
    devices,
    normed_input,
    projection_output_gradient,
    query,
    key,
    value,
    frozen_output_gradient,
    query_down_weight,
    query_up_weight,
    key_down_weight,
    key_up_weight,
    value_down_weight,
    value_up_weight,
    output_down_weight,
    output_up_weight,
):
    x = normed_input[0]
    pog = projection_output_gradient[0]
    tok, width = x.shape
    peers = GROUP // 2 // tok
    count = lax.axis_size("ctx")
    groups = [list(range(s, s + peers)) for s in range(0, count, peers)]
    down_t = output_down_weight.T
    ahead = [(s, ((s ^ MIRROR) + peers) % count) for s in range(count)]
    behind = [((s + peers) % count, s) for s in range(count)]
    near = count == 2 * peers

    def swap(array):
        return lax.all_to_all(array, "ctx", 0, 0, axis_index_groups=groups)

    cores = lax.axis_size("dp")

    def exchange(parts):
        moved = [parts[0]]
        for k in range(1, peers):
            pairs = [(c * cores + d, (c ^ ORDERS[d % 2][k]) * cores + d) for c in range(count) for d in range(cores)]
            moved.append(lax.ppermute(parts[k], ("ctx", "dp"), pairs))
        return tuple(moved)

    weights = (query_down_weight.T, key_down_weight.T, value_down_weight.T, output_up_weight, down_t)
    sources = (query[0], key[0], value[0], x, pog, frozen_output_gradient[0]) + weights
    packed = call(
        pack_kernel,
        (jax.ShapeDtypeStruct((4 * tok + 32, HEAD_WIDTH), BF16),) * peers
        + (jax.ShapeDtypeStruct((4 * tok, HEAD_WIDTH), BF16),) * peers,
        sources,
        tuple(pltpu.VMEM(source.shape, BF16) for source in sources) + (pltpu.SemaphoreType.DMA((19,)),),
        flops=1 << 28,
        moved=4 << 20,
        far=len(sources),
        limit=VMEM_PACK,
    )
    firsts, seconds = packed[:peers], packed[peers:]
    firsts = exchange(firsts)
    cross = call(
        assemble_kernel,
        jax.ShapeDtypeStruct((peers, 2 * tok + 16, HEAD_WIDTH), BF16),
        firsts,
        moved=2 << 20,
    )
    cross = lax.ppermute(cross, "ctx", ahead)
    seconds = exchange(seconds)
    length = peers * tok
    ups = (query_up_weight, key_up_weight, value_up_weight, down_t)

    def scratch(keys):
        return (
            pltpu.VMEM((length, HEAD_WIDTH), BF16),
            pltpu.VMEM((length, HEAD_WIDTH), BF16),
            pltpu.VMEM((keys, 2 * HEAD_WIDTH), BF16),
            pltpu.VMEM((keys, 2 * HEAD_WIDTH), BF16),
            pltpu.VMEM((16, keys), F32),
        )

    pairs = length * length
    first_terms, head_f, low, low_tokens = call(
        first_kernel,
        (
            jax.ShapeDtypeStruct((peers, 32, HEAD_WIDTH), F32),
            jax.ShapeDtypeStruct((32, HEAD_WIDTH), F32),
            jax.ShapeDtypeStruct((peers, 32, HEAD_WIDTH), BF16),
            jax.ShapeDtypeStruct((length, HEAD_WIDTH), BF16),
        ),
        firsts + ups,
        scratch(length),
        flops=pairs * 6 * 256,
        moved=3 << 20,
        exps=pairs // 2,
    )
    terms, heads = call(
        functools.partial(second_kernel, near),
        (
            jax.ShapeDtypeStruct((count, 32, HEAD_WIDTH) if near else (peers, 48, HEAD_WIDTH), BF16),
            jax.ShapeDtypeStruct((64, HEAD_WIDTH), F32),
        ),
        seconds + (cross, low, low_tokens, first_terms, head_f) + ups,
        scratch(2 * length),
        flops=3 * pairs * 6 * 256,
        moved=3 << 20,
        exps=3 * pairs // 2,
    )
    if near:
        back = ()
        terms = lax.all_to_all(terms, "ctx", 0, 0)
    else:
        terms = swap(terms)
        back = (lax.ppermute(jnp.sum(terms[:, 32:, :].astype(F32), axis=0), "ctx", behind),)
    wide = width // HEAD_WIDTH
    share = HALF_HEADS * 64 // devices
    direct = devices == wide and share % 16 == 0
    if direct:
        shapes = (jax.ShapeDtypeStruct((wide, 32 + share, HEAD_WIDTH), BF16),)
    else:
        shapes = (
            jax.ShapeDtypeStruct((wide, 32, HEAD_WIDTH), BF16),
            jax.ShapeDtypeStruct((HALF_HEADS, 64, HEAD_WIDTH), BF16),
        )
    parts = call(
        functools.partial(product_kernel, direct, near),
        shapes,
        (terms,) + back + (x, pog, heads),
        flops=2 * 32 * tok * width,
        moved=3 << 20,
    )
    rows = [wide * 32 // devices, share]
    if direct:
        parts = parts[0]
    else:
        parts = jnp.concatenate(
            [part.reshape(devices, n, HEAD_WIDTH) for part, n in zip(parts, rows)], axis=1)
    parts = lax.all_to_all(parts, ("ctx", "dp"), 0, 0)
    paired = direct and lax.axis_size("dp") == 2
    shared = call(
        share_kernel,
        jax.ShapeDtypeStruct((count if paired else devices,) + parts.shape[1:], BF16),
        (parts,),
        moved=1 << 20,
    )
    if paired:
        mine = lax.all_to_all(shared, "ctx", 0, 0)
        gathered = (mine, lax.ppermute(mine, "dp", [(0, 1), (1, 0)]))
    else:
        gathered = (lax.all_to_all(shared, ("ctx", "dp"), 0, 0),)
    if not direct:
        gathered = (
            gathered[0][:, :rows[0]].reshape(wide, 32, HEAD_WIDTH),
            gathered[0][:, rows[0]:].reshape(HALF_HEADS, 64, HEAD_WIDTH),
        )
    kind = "paired" if paired else "whole" if direct else "parts"
    narrow = SHIFT_HEADS * HEAD_WIDTH
    columns = (width, narrow, width, narrow, width, narrow, narrow, width)
    outs = call(
        functools.partial(finish_kernel, kind),
        tuple(jax.ShapeDtypeStruct((ADAPTER_RANK, n), F32) for n in columns),
        gathered,
        moved=2 << 20,
    )
    return tuple(out.T if i in (0, 2, 4, 6) else out for i, out in enumerate(outs))


def solution(mesh):
    placed = (P("dp", "ctx", None),) * 6 + (P(),) * 8
    return jax.shard_map(
        functools.partial(per_device, mesh.size),
        mesh=mesh,
        in_specs=placed,
        out_specs=(P(),) * 8,
        check_vma=False,
    )
```

```python
import functools
import math

import jax
import jax.numpy as jnp
from jax import lax
from jax.experimental import pallas as pl
from jax.experimental.pallas import tpu as pltpu
from jax.sharding import PartitionSpec as P

SHIFT_HEADS = 16
HEAD_WIDTH = 128
ADAPTER_RANK = 8
GROUP = 2048

HALF_HEADS = SHIFT_HEADS // 2
HALF_COLUMNS = HALF_HEADS * HEAD_WIDTH
SCALE = HEAD_WIDTH ** (-0.5)
LOG2E = math.log2(math.e)
MASKED = -1e30
F32 = jnp.float32
BF16 = jnp.bfloat16
NT = (((1,), (1,)), ((), ()))
ORDERS = ((0, 1, 6, 2, 5, 4, 3, 7), (0, 6, 1, 5, 2, 3, 4, 7))
BLOCK = 256
VMEM_LIMIT = 24 * 1024 * 1024
VMEM_PACK = 56 * 1024 * 1024


def dot(a, b):
    return jnp.dot(a, b, preferred_element_type=F32)


def dot_nt(a, b):
    return lax.dot_general(a, b, NT, preferred_element_type=F32)


def call(kernel, out_shape, inputs, scratch=(), flops=0, moved=0, exps=0, limit=VMEM_LIMIT, far=0):
    return pl.pallas_call(
        kernel,
        out_shape=out_shape,
        in_specs=[pl.BlockSpec(memory_space=pltpu.HBM if i < far else pltpu.VMEM) for i in range(len(inputs))],
        out_specs=jax.tree.map(lambda _: pl.BlockSpec(memory_space=pltpu.VMEM), out_shape),
        scratch_shapes=list(scratch),
        compiler_params=pltpu.CompilerParams(vmem_limit_bytes=limit),
        cost_estimate=pl.CostEstimate(flops=flops, bytes_accessed=moved, transcendentals=exps),
    )(*inputs)


MIRROR = HALF_HEADS // 2


def place():
    index = lax.axis_index("ctx")
    return lax.rem(lax.div(index, HALF_HEADS), 2), lax.rem(index, HALF_HEADS)


def partners():
    _, slot = place()
    core = lax.rem(lax.axis_index("dp"), 2)
    return [jnp.bitwise_xor(slot, jnp.where(core == 0, a, b)) for a, b in zip(*ORDERS)]


def rows_at(index):
    return pl.ds(pl.multiple_of(index * HEAD_WIDTH, HEAD_WIDTH), HEAD_WIDTH)


def head_columns(ref, head):
    return ref[:, pl.ds(pl.multiple_of(head * HEAD_WIDTH, HEAD_WIDTH), HEAD_WIDTH)]


def tokens_first(rows):
    pad = jnp.zeros((HEAD_WIDTH - rows.shape[0], rows.shape[1]), F32)
    return jnp.transpose(jnp.concatenate([rows, pad], axis=0))


def pack_kernel(q, k, v, x, pog, f, qd, kd, vd, ou, od, *refs):
    outs, bufs, sems = refs[:-12], refs[-12:-1], refs[-1]
    firsts, seconds = outs[:HALF_HEADS], outs[HALF_HEADS:]
    qs, ks, vs, xs, ps, fs, qds, kds, vds, ous, ods = bufs
    odd, _ = place()
    tok, width = x.shape
    chunks = 4
    step = width // chunks
    sources = (q, k, v, x, pog, f, qd, kd, vd, ou, od)
    whole = {i: pltpu.make_async_copy(sources[i], bufs[i], sems.at[i]) for i in (0, 1, 2, 5, 6, 7, 8, 9, 10)}
    wide = []
    for c in range(chunks):
        columns = pl.ds(c * step, step)
        wide.append([pltpu.make_async_copy(sources[i].at[:, columns], bufs[i].at[:, columns], sems.at[11 + (i - 3) * chunks + c])
                     for i in (3, 4)])
    for i in (6, 7, 8, 9):
        whole[i].start()
    for pair in wide[:2]:
        for copy in pair:
            copy.start()
    for i in (0, 1, 2):
        whole[i].start()
    for pair in wide[2:]:
        for copy in pair:
            copy.start()
    for i in (10, 5):
        whole[i].start()
    for i in (6, 7, 8, 9):
        whole[i].wait()
    gap = jnp.zeros((8, width), BF16)
    down = jnp.concatenate([qds[...], gap, kds[...], vds[...]], axis=0)
    upper = jnp.concatenate([gap, ous[...], gap, gap], axis=0)
    low = jnp.zeros((tok, 32), F32)
    peers = partners()
    spots = ((0, 0, 0), (1, 2 * tok + 32, 2 * tok), (2, 3 * tok + 32, 3 * tok))
    for c in range(chunks):
        columns = slice(c * step, (c + 1) * step)
        wide[c][0].wait()
        low += dot_nt(xs[:, columns], down[:, columns])
        wide[c][1].wait()
        low += dot_nt(ps[:, columns], upper[:, columns])
        if c > 0:
            i, at, late = spots[c - 1]
            whole[i].wait()
            spread(bufs[i], odd, peers, firsts, at, seconds, late)
    low_b = jnp.transpose(jnp.concatenate([low, jnp.zeros((tok, HEAD_WIDTH - 32), F32)], axis=1))[:32].astype(BF16)
    by_token = low.astype(BF16)
    columns = od.shape[1]
    whole[10].wait()
    up = jnp.concatenate([jnp.zeros((8, columns), BF16), ods[...], jnp.zeros((16, columns), BF16)], axis=0)
    raised = dot(by_token, up)
    whole[5].wait()
    fs[...] = (fs[...].astype(F32) + raised).astype(BF16)
    spread(fs, odd, peers, firsts, tok, seconds, tok)
    for first in firsts:
        first[2 * tok:2 * tok + 32, :] = low_b


def spread(array, odd, peers, firsts, at, seconds, late):
    tok = array.shape[0]
    for peer, first, second in zip(peers, firsts, seconds):
        first[at:at + tok, :] = head_columns(array, peer + HALF_HEADS * odd)
        second[late:late + tok, :] = head_columns(array, second_head(peer) + HALF_HEADS * (1 - odd))


def second_head(peer):
    return jnp.bitwise_xor(peer, MIRROR)


def keep_kernel(part, out):
    out[...] = part[...]


def assemble_kernel(*refs):
    parts, cross = refs[:-1], refs[-1]
    for peer, part in zip(partners(), parts):
        cross[peer] = part[2 * HEAD_WIDTH + 16:, :]


def attend(head, lead, low, qu, ku, vu, od, queries, grads, kext, vext, sums, emit):
    tok = HEAD_WIDTH
    length = queries.shape[0]
    peers = length // tok
    low = [low[p] for p in range(peers)]
    low = jnp.concatenate(low, axis=1).astype(F32)
    low_q = low[0:8].astype(BF16)
    low_o = low[8:16].astype(BF16)
    up_q = head_columns(qu, head)
    up_k = head_columns(ku, head)
    up_v = head_columns(vu, head)
    down = head_columns(od, head)
    total = lead + length
    sums[...] = jnp.zeros_like(sums)
    bq = jnp.zeros((8, HEAD_WIDTH), F32)
    bk, bv, ao = bq, bq, bq
    factor = SCALE * LOG2E
    rows_of = lax.broadcasted_iota(jnp.int32, (BLOCK, BLOCK), 0)
    columns_of = lax.broadcasted_iota(jnp.int32, (BLOCK, BLOCK), 1)
    causal = columns_of <= rows_of
    per = BLOCK // tok
    pairs = []
    def scored(b):
        qb = queries[b * BLOCK:(b + 1) * BLOCK, :]
        gb = grads[b * BLOCK:(b + 1) * BLOCK, :]
        past = lead + b * BLOCK
        reach = past + BLOCK
        scores = dot_nt(qb, kext[:reach, :tok])
        dweights = dot_nt(gb, vext[:reach, :tok])
        return qb, gb, past, reach, scores, dweights

    def softened(scores, past):
        diagonal = jnp.where(causal, scores[:, past:], MASKED)
        scores = jnp.concatenate([scores[:, :past], diagonal], axis=1) if past else diagonal
        summit = jnp.max(scores, axis=1, keepdims=True)
        e = jnp.exp2((scores - summit) * factor)
        return e, 1.0 / jnp.sum(e, axis=1, keepdims=True)

    count = length // BLOCK
    ahead = scored(0)
    for b in range(count):
        qb, gb, past, reach, scores, dweights = ahead
        if b + 1 < count:
            ahead = scored(b + 1)
        e, inv = softened(scores, past)
        p = e.astype(BF16)
        mixed = dot(p, vext[:reach, :])
        output = mixed[:, :tok] * inv
        gs = (gb.astype(F32) * inv).astype(BF16)
        sums[8:16, :reach] += dot(dot_nt(up_v, gs).astype(BF16), p)
        delta = jnp.sum(gb.astype(F32) * output, axis=1, keepdims=True)
        ds = (e * (dweights - delta)).astype(BF16)
        dmixed = dot(ds, kext[:reach, :])
        row_scale = inv * SCALE
        dq = (dmixed[:, :tok] * row_scale).astype(BF16)
        qs = (qb.astype(F32) * row_scale).astype(BF16)
        ob = output.astype(BF16)
        sums[0:8, :reach] += dot(dot_nt(up_k, qs).astype(BF16), ds)
        bk += dot(jnp.transpose(dmixed[:, tok:])[16:24].astype(BF16), qs)
        bv += dot(jnp.transpose(mixed[:, tok:])[24:32].astype(BF16), gs)
        bq += dot(low_q[:, b * BLOCK:(b + 1) * BLOCK], dq)
        ao += dot(low_o[:, b * BLOCK:(b + 1) * BLOCK], ob)
        low_dq = dot_nt(up_q, dq)
        out_red = dot_nt(down, ob)
        pair = jnp.concatenate([low_dq, out_red], axis=0)
        pairs += [pair[:, i * tok:(i + 1) * tok] for i in range(per)]
    for p in range(peers):
        at = lead + p * tok
        own = jnp.concatenate([pairs[p], sums[:, at:at + tok]], axis=0)
        emit(p, own, sums[:, p * tok:(p + 1) * tok] if lead else None)
    return jnp.concatenate([bq, bk, bv, ao], axis=0)


def first_kernel(*refs):
    parts, refs = refs[:HALF_HEADS], refs[HALF_HEADS:]
    qu, ku, vu, od, terms, head, low, token_low, queries, grads, kext, vext, sums = refs
    odd, slot = place()
    tok = HEAD_WIDTH
    for peer, part in zip(partners(), parts):
        at = rows_at(peer)
        queries[at, :] = part[:tok, :]
        grads[at, :] = part[tok:2 * tok, :]
        rows = part[2 * tok:2 * tok + 32, :]
        low[peer] = rows
        t = tokens_first(rows.astype(F32)).astype(BF16)
        token_low[at, :] = t
        kext[at, :tok] = part[2 * tok + 32:3 * tok + 32, :]
        vext[at, :tok] = part[3 * tok + 32:, :]
        kext[at, tok:] = t
        vext[at, tok:] = t

    def emit(p, own, previous):
        terms[p] = own

    head[...] = attend(slot + HALF_HEADS * odd, 0, low, qu, ku, vu, od, queries, grads, kext, vext, sums, emit)


def second_kernel(near, *refs):
    parts, refs = refs[:HALF_HEADS], refs[HALF_HEADS:]
    cross, low, token_low, first_terms, head_f, qu, ku, vu, od, terms, heads, queries, grads, kext, vext, sums = refs
    odd, slot = place()
    tok = HEAD_WIDTH
    length = token_low.shape[0]
    for peer, part in zip(partners(), parts):
        at = rows_at(peer)
        late = rows_at(peer + HALF_HEADS)
        queries[at, :] = part[:tok, :]
        grads[at, :] = part[tok:2 * tok, :]
        kext[late, :tok] = part[2 * tok:3 * tok, :]
        vext[late, :tok] = part[3 * tok:, :]
    kext[length:, tok:] = token_low[...]
    vext[length:, tok:] = token_low[...]
    for p in range(HALF_HEADS):
        at = slice(p * tok, (p + 1) * tok)
        rows = jnp.concatenate([jnp.zeros((16, tok), F32), cross[p, :16, :].astype(F32)], axis=0)
        t = tokens_first(rows).astype(BF16)
        kext[at, :tok] = cross[p, 16:16 + tok, :]
        vext[at, :tok] = cross[p, 16 + tok:, :]
        kext[at, tok:] = t
        vext[at, tok:] = t
    mine = odd * HALF_HEADS
    other = HALF_HEADS - mine

    def emit(p, own, previous):
        own = own + first_terms[p]
        if near:
            terms[mine + p] = own.astype(BF16)
            terms[other + p] = jnp.concatenate([jnp.zeros((16, tok), F32), previous], axis=0).astype(BF16)
        else:
            terms[p] = jnp.concatenate([own, previous], axis=0).astype(BF16)

    head_s = attend(second_head(slot) + HALF_HEADS * (1 - odd), length, low, qu, ku, vu, od, queries, grads, kext, vext, sums, emit)
    heads[:32, :] = head_f[...]
    heads[32:, :] = head_s


def product_kernel(kind, near, terms, *refs):
    own = jnp.sum(terms[:, :32, :].astype(F32), axis=0)
    mixed = own[16:32]
    if not near:
        mixed = mixed + refs[0][...]
        refs = refs[1:]
    x, pog, heads, *outs = refs
    left = jnp.concatenate([own[0:8], mixed], axis=0).astype(BF16)
    right = own[8:16].astype(BF16)
    wide = x.shape[1] // HEAD_WIDTH
    head = heads[...].astype(BF16)
    odd, slot = place()
    step = 4
    zero = lax.axis_index("dp") == 0

    def put(pair, rows, first, second):
        outs[0][pair, rows, :] = jnp.where(zero, first, second)
        outs[1][pair, rows, :] = jnp.where(zero, second, first)

    for c in range(0, wide, step):
        columns = slice(c * HEAD_WIDTH, (c + step) * HEAD_WIDTH)
        a = jnp.concatenate([dot(left, x[:, columns]), dot(right, pog[:, columns])], axis=0).astype(BF16)
        a = [a[:, i * HEAD_WIDTH:(i + 1) * HEAD_WIDTH] for i in range(step)]
        for i in range(step):
            if kind != "paired":
                outs[0][c + i, :32, :] = a[i]
            elif i % 2 == 0:
                put((c + i) // 2, slice(0, 32), a[i], a[i + 1])
    spots = ((slot, odd), (second_head(slot), 1 - odd))
    per = wide // HALF_HEADS
    share = 64 // per
    if kind == "parts":
        outs[1][...] = jnp.zeros(outs[1].shape, BF16)
        for i, (where, half) in enumerate(spots):
            outs[1][where, pl.ds(pl.multiple_of(32 * half, 32), 32), :] = head[32 * i:32 * i + 32]
        return
    for out in outs:
        out[:, 32:, :] = jnp.zeros((out.shape[0], share, HEAD_WIDTH), BF16)
    for i in range(per):
        where, half = spots[2 * i // per]
        at = where * per + half * (per // 2) + i % (per // 2)
        if kind != "paired":
            outs[0][at, 32:, :] = head[i * share:(i + 1) * share]
        elif i % 2 == 0:
            put(lax.div(at, 2), slice(32, 32 + share), head[i * share:(i + 1) * share], head[(i + 1) * share:(i + 2) * share])


def add_kernel(a, b, out):
    out[...] = (a[...].astype(F32) + b[...].astype(F32)).astype(BF16)


def share_kernel(parts, out):
    summed = jnp.sum(parts[...].astype(F32), axis=0).astype(BF16)
    out[...] = jnp.broadcast_to(summed[None], out.shape)


def finish_kernel(kind, *refs):
    outs = refs[-8:]
    refs = refs[:-8]
    wide = outs[0].shape[1] // HEAD_WIDTH
    per = wide // HALF_HEADS
    zero = lax.axis_index("dp") == 0

    def chunk(c):
        if kind == "paired":
            mine, other = refs[0][c // 2], refs[1][c // 2]
            return jnp.where(zero, mine, other) if c % 2 == 0 else jnp.where(zero, other, mine)
        return refs[0][c]

    head = []
    for c in range(wide):
        rows = chunk(c).astype(F32)
        for i, o in enumerate((0, 2, 4, 7)):
            outs[o][:, c * HEAD_WIDTH:(c + 1) * HEAD_WIDTH] = rows[8 * i:8 * i + 8]
        if kind != "parts":
            head.append(rows[32:])
    for j in range(HALF_HEADS):
        if kind == "parts":
            rows = refs[1][j].astype(F32)
        else:
            rows = jnp.concatenate(head[j * per:(j + 1) * per], axis=0)
        for half in range(2):
            at = (j + half * HALF_HEADS) * HEAD_WIDTH
            for i, o in enumerate((1, 3, 5, 6)):
                outs[o][:, at:at + HEAD_WIDTH] = rows[32 * half + 8 * i:32 * half + 8 * i + 8]


def per_device(
    devices,
    normed_input,
    projection_output_gradient,
    query,
    key,
    value,
    frozen_output_gradient,
    query_down_weight,
    query_up_weight,
    key_down_weight,
    key_up_weight,
    value_down_weight,
    value_up_weight,
    output_down_weight,
    output_up_weight,
):
    x = normed_input[0]
    pog = projection_output_gradient[0]
    tok, width = x.shape
    peers = GROUP // 2 // tok
    count = lax.axis_size("ctx")
    groups = [list(range(s, s + peers)) for s in range(0, count, peers)]
    down_t = output_down_weight.T
    ahead = [(s, ((s ^ MIRROR) + peers) % count) for s in range(count)]
    behind = [((s + peers) % count, s) for s in range(count)]
    near = count == 2 * peers

    def swap(array):
        return lax.all_to_all(array, "ctx", 0, 0, axis_index_groups=groups)

    cores = lax.axis_size("dp")

    def exchange(parts):
        moved = [parts[0]]
        for k in range(1, peers):
            pairs = [(c * cores + d, (c ^ ORDERS[d % 2][k]) * cores + d) for c in range(count) for d in range(cores)]
            moved.append(lax.ppermute(parts[k], ("ctx", "dp"), pairs))
        return tuple(moved)

    weights = (query_down_weight.T, key_down_weight.T, value_down_weight.T, output_up_weight, down_t)
    sources = (query[0], key[0], value[0], x, pog, frozen_output_gradient[0]) + weights
    packed = call(
        pack_kernel,
        (jax.ShapeDtypeStruct((4 * tok + 32, HEAD_WIDTH), BF16),) * peers
        + (jax.ShapeDtypeStruct((4 * tok, HEAD_WIDTH), BF16),) * peers,
        sources,
        tuple(pltpu.VMEM(source.shape, BF16) for source in sources) + (pltpu.SemaphoreType.DMA((19,)),),
        flops=1 << 28,
        moved=4 << 20,
        far=len(sources),
        limit=VMEM_PACK,
    )
    firsts, seconds = packed[:peers], packed[peers:]
    firsts = (call(keep_kernel, jax.ShapeDtypeStruct(firsts[0].shape, BF16), firsts[:1]),) + tuple(firsts[1:])
    firsts = exchange(firsts)
    cross = call(
        assemble_kernel,
        jax.ShapeDtypeStruct((peers, 2 * tok + 16, HEAD_WIDTH), BF16),
        firsts,
        moved=2 << 20,
    )
    cross = lax.ppermute(cross, "ctx", ahead)
    seconds = exchange(seconds)
    length = peers * tok
    ups = (query_up_weight, key_up_weight, value_up_weight, down_t)

    def scratch(keys):
        return (
            pltpu.VMEM((length, HEAD_WIDTH), BF16),
            pltpu.VMEM((length, HEAD_WIDTH), BF16),
            pltpu.VMEM((keys, 2 * HEAD_WIDTH), BF16),
            pltpu.VMEM((keys, 2 * HEAD_WIDTH), BF16),
            pltpu.VMEM((16, keys), F32),
        )

    pairs = length * length
    first_terms, head_f, low, low_tokens = call(
        first_kernel,
        (
            jax.ShapeDtypeStruct((peers, 32, HEAD_WIDTH), F32),
            jax.ShapeDtypeStruct((32, HEAD_WIDTH), F32),
            jax.ShapeDtypeStruct((peers, 32, HEAD_WIDTH), BF16),
            jax.ShapeDtypeStruct((length, HEAD_WIDTH), BF16),
        ),
        firsts + ups,
        scratch(length),
        flops=pairs * 6 * 256,
        moved=3 << 20,
        exps=pairs // 2,
    )
    terms, heads = call(
        functools.partial(second_kernel, near),
        (
            jax.ShapeDtypeStruct((count, 32, HEAD_WIDTH) if near else (peers, 48, HEAD_WIDTH), BF16),
            jax.ShapeDtypeStruct((64, HEAD_WIDTH), F32),
        ),
        seconds + (cross, low, low_tokens, first_terms, head_f) + ups,
        scratch(2 * length),
        flops=3 * pairs * 6 * 256,
        moved=3 << 20,
        exps=3 * pairs // 2,
    )
    if near:
        back = ()
        terms = lax.all_to_all(terms, "ctx", 0, 0)
    else:
        terms = swap(terms)
        back = (lax.ppermute(jnp.sum(terms[:, 32:, :].astype(F32), axis=0), "ctx", behind),)
    wide = width // HEAD_WIDTH
    share = HALF_HEADS * 64 // devices
    direct = devices == wide and share % 16 == 0
    paired = direct and lax.axis_size("dp") == 2
    kind = "paired" if paired else "whole" if direct else "parts"
    other_core = [(0, 1), (1, 0)]
    if paired:
        shapes = (jax.ShapeDtypeStruct((count, 32 + share, HEAD_WIDTH), BF16),) * 2
    elif direct:
        shapes = (jax.ShapeDtypeStruct((wide, 32 + share, HEAD_WIDTH), BF16),)
    else:
        shapes = (
            jax.ShapeDtypeStruct((wide, 32, HEAD_WIDTH), BF16),
            jax.ShapeDtypeStruct((HALF_HEADS, 64, HEAD_WIDTH), BF16),
        )
    parts = call(
        functools.partial(product_kernel, kind, near),
        shapes,
        (terms,) + back + (x, pog, heads),
        flops=2 * 32 * tok * width,
        moved=3 << 20,
    )
    rows = [wide * 32 // devices, share]
    if paired:
        theirs = lax.ppermute(parts[1], "dp", other_core)
        parts = call(add_kernel, shapes[0], (parts[0], theirs), moved=1 << 20)
        parts = lax.all_to_all(parts, "ctx", 0, 0)
    else:
        if direct:
            parts = parts[0]
        else:
            parts = jnp.concatenate(
                [part.reshape(devices, n, HEAD_WIDTH) for part, n in zip(parts, rows)], axis=1)
        parts = lax.all_to_all(parts, ("ctx", "dp"), 0, 0)
    shared = call(
        share_kernel,
        jax.ShapeDtypeStruct(parts.shape, BF16),
        (parts,),
        moved=1 << 20,
    )
    if paired:
        mine = lax.all_to_all(shared, "ctx", 0, 0)
        gathered = (mine, lax.ppermute(mine, "dp", other_core))
    else:
        gathered = (lax.all_to_all(shared, ("ctx", "dp"), 0, 0),)
    if not direct:
        gathered = (
            gathered[0][:, :rows[0]].reshape(wide, 32, HEAD_WIDTH),
            gathered[0][:, rows[0]:].reshape(HALF_HEADS, 64, HEAD_WIDTH),
        )
    narrow = SHIFT_HEADS * HEAD_WIDTH
    columns = (width, narrow, width, narrow, width, narrow, narrow, width)
    outs = call(
        functools.partial(finish_kernel, kind),
        tuple(jax.ShapeDtypeStruct((ADAPTER_RANK, n), F32) for n in columns),
        gathered,
        moved=2 << 20,
    )
    return tuple(out.T if i in (0, 2, 4, 6) else out for i, out in enumerate(outs))


def solution(mesh):
    placed = (P("dp", "ctx", None),) * 6 + (P(),) * 8
    return jax.shard_map(
        functools.partial(per_device, mesh.size),
        mesh=mesh,
        in_specs=placed,
        out_specs=(P(),) * 8,
        check_vma=False,
    )
```

```python
import functools
import math

import jax
import jax.numpy as jnp
from jax import lax
from jax.experimental import pallas as pl
from jax.experimental.pallas import tpu as pltpu
from jax.sharding import PartitionSpec as P

SHIFT_HEADS = 16
HEAD_WIDTH = 128
ADAPTER_RANK = 8
GROUP = 2048

HALF_HEADS = SHIFT_HEADS // 2
HALF_COLUMNS = HALF_HEADS * HEAD_WIDTH
SCALE = HEAD_WIDTH ** (-0.5)
LOG2E = math.log2(math.e)
MASKED = -1e30
F32 = jnp.float32
BF16 = jnp.bfloat16
NT = (((1,), (1,)), ((), ()))
ORDERS = ((0, 1, 6, 2, 5, 4, 3, 7), (0, 6, 1, 5, 2, 3, 4, 7))
LATER = ((0, 1, 2, 3, 7, 4, 5, 6), (0, 2, 1, 3, 7, 4, 6, 5))
BLOCK = 256
VMEM_LIMIT = 24 * 1024 * 1024
VMEM_PACK = 56 * 1024 * 1024


def dot(a, b):
    return jnp.dot(a, b, preferred_element_type=F32)


def dot_nt(a, b):
    return lax.dot_general(a, b, NT, preferred_element_type=F32)


def call(kernel, out_shape, inputs, scratch=(), flops=0, moved=0, exps=0, limit=VMEM_LIMIT, far=0):
    return pl.pallas_call(
        kernel,
        out_shape=out_shape,
        in_specs=[pl.BlockSpec(memory_space=pltpu.HBM if i < far else pltpu.VMEM) for i in range(len(inputs))],
        out_specs=jax.tree.map(lambda _: pl.BlockSpec(memory_space=pltpu.VMEM), out_shape),
        scratch_shapes=list(scratch),
        compiler_params=pltpu.CompilerParams(vmem_limit_bytes=limit),
        cost_estimate=pl.CostEstimate(flops=flops, bytes_accessed=moved, transcendentals=exps),
    )(*inputs)


MIRROR = HALF_HEADS // 2


def place():
    index = lax.axis_index("ctx")
    return lax.rem(lax.div(index, HALF_HEADS), 2), lax.rem(index, HALF_HEADS)


def partners(orders=ORDERS):
    _, slot = place()
    core = lax.rem(lax.axis_index("dp"), 2)
    return [jnp.bitwise_xor(slot, jnp.where(core == 0, a, b)) for a, b in zip(*orders)]


def rows_at(index):
    return pl.ds(pl.multiple_of(index * HEAD_WIDTH, HEAD_WIDTH), HEAD_WIDTH)


def head_columns(ref, head):
    return ref[:, pl.ds(pl.multiple_of(head * HEAD_WIDTH, HEAD_WIDTH), HEAD_WIDTH)]


def tokens_first(rows):
    pad = jnp.zeros((HEAD_WIDTH - rows.shape[0], rows.shape[1]), F32)
    return jnp.transpose(jnp.concatenate([rows, pad], axis=0))


def pack_kernel(q, k, v, x, pog, f, qd, kd, vd, ou, od, *refs):
    outs, bufs, sems = refs[:-12], refs[-12:-1], refs[-1]
    firsts, seconds = outs[:HALF_HEADS], outs[HALF_HEADS:]
    qs, ks, vs, xs, ps, fs, qds, kds, vds, ous, ods = bufs
    odd, _ = place()
    tok, width = x.shape
    chunks = 4
    step = width // chunks
    sources = (q, k, v, x, pog, f, qd, kd, vd, ou, od)
    whole = {i: pltpu.make_async_copy(sources[i], bufs[i], sems.at[i]) for i in (0, 1, 2, 5, 6, 7, 8, 9, 10)}
    wide = []
    for c in range(chunks):
        columns = pl.ds(c * step, step)
        wide.append([pltpu.make_async_copy(sources[i].at[:, columns], bufs[i].at[:, columns], sems.at[11 + (i - 3) * chunks + c])
                     for i in (3, 4)])
    for i in (6, 7, 8, 9):
        whole[i].start()
    for pair in wide[:2]:
        for copy in pair:
            copy.start()
    for i in (0, 1, 2):
        whole[i].start()
    for pair in wide[2:]:
        for copy in pair:
            copy.start()
    for i in (10, 5):
        whole[i].start()
    for i in (6, 7, 8, 9):
        whole[i].wait()
    gap = jnp.zeros((8, width), BF16)
    down = jnp.concatenate([qds[...], gap, kds[...], vds[...]], axis=0)
    upper = jnp.concatenate([gap, ous[...], gap, gap], axis=0)
    low = jnp.zeros((tok, 32), F32)
    peers = partners()
    spots = ((0, 0, 0), (1, 2 * tok + 32, 2 * tok), (2, 3 * tok + 32, 3 * tok))
    for c in range(chunks):
        columns = slice(c * step, (c + 1) * step)
        wide[c][0].wait()
        low += dot_nt(xs[:, columns], down[:, columns])
        wide[c][1].wait()
        low += dot_nt(ps[:, columns], upper[:, columns])
        if c > 0:
            i, at, late = spots[c - 1]
            whole[i].wait()
            spread(bufs[i], odd, peers, firsts, at, seconds, late)
    low_b = jnp.transpose(jnp.concatenate([low, jnp.zeros((tok, HEAD_WIDTH - 32), F32)], axis=1))[:32].astype(BF16)
    by_token = low.astype(BF16)
    columns = od.shape[1]
    whole[10].wait()
    up = jnp.concatenate([jnp.zeros((8, columns), BF16), ods[...], jnp.zeros((16, columns), BF16)], axis=0)
    raised = dot(by_token, up)
    whole[5].wait()
    fs[...] = (fs[...].astype(F32) + raised).astype(BF16)
    spread(fs, odd, peers, firsts, tok, seconds, tok)
    for first in firsts:
        first[2 * tok:2 * tok + 32, :] = low_b


def spread(array, odd, peers, firsts, at, seconds, late):
    tok = array.shape[0]
    for peer, first in zip(peers, firsts):
        first[at:at + tok, :] = head_columns(array, peer + HALF_HEADS * odd)
    for peer, second in zip(partners(LATER), seconds):
        second[late:late + tok, :] = head_columns(array, second_head(peer) + HALF_HEADS * (1 - odd))


def second_head(peer):
    return jnp.bitwise_xor(peer, MIRROR)


def keep_kernel(part, out):
    out[...] = part[...]


def assemble_kernel(*refs):
    parts, cross = refs[:-1], refs[-1]
    for peer, part in zip(partners(), parts):
        cross[peer] = part[2 * HEAD_WIDTH + 16:, :]


def attend(head, lead, low, qu, ku, vu, od, queries, grads, kext, vext, sums, emit):
    tok = HEAD_WIDTH
    length = queries.shape[0]
    peers = length // tok
    low = [low[p] for p in range(peers)]
    low = jnp.concatenate(low, axis=1).astype(F32)
    low_q = low[0:8].astype(BF16)
    low_o = low[8:16].astype(BF16)
    up_q = head_columns(qu, head)
    up_k = head_columns(ku, head)
    up_v = head_columns(vu, head)
    down = head_columns(od, head)
    total = lead + length
    sums[...] = jnp.zeros_like(sums)
    bq = jnp.zeros((8, HEAD_WIDTH), F32)
    bk, bv, ao = bq, bq, bq
    factor = SCALE * LOG2E
    rows_of = lax.broadcasted_iota(jnp.int32, (BLOCK, BLOCK), 0)
    columns_of = lax.broadcasted_iota(jnp.int32, (BLOCK, BLOCK), 1)
    causal = columns_of <= rows_of
    per = BLOCK // tok
    pairs = []
    def scored(b):
        qb = queries[b * BLOCK:(b + 1) * BLOCK, :]
        gb = grads[b * BLOCK:(b + 1) * BLOCK, :]
        past = lead + b * BLOCK
        reach = past + BLOCK
        scores = dot_nt(qb, kext[:reach, :tok])
        dweights = dot_nt(gb, vext[:reach, :tok])
        return qb, gb, past, reach, scores, dweights

    def softened(scores, past):
        diagonal = jnp.where(causal, scores[:, past:], MASKED)
        scores = jnp.concatenate([scores[:, :past], diagonal], axis=1) if past else diagonal
        summit = jnp.max(scores, axis=1, keepdims=True)
        e = jnp.exp2((scores - summit) * factor)
        return e, 1.0 / jnp.sum(e, axis=1, keepdims=True)

    count = length // BLOCK
    ahead = scored(0)
    for b in range(count):
        qb, gb, past, reach, scores, dweights = ahead
        if b + 1 < count:
            ahead = scored(b + 1)
        e, inv = softened(scores, past)
        p = e.astype(BF16)
        mixed = dot(p, vext[:reach, :])
        output = mixed[:, :tok] * inv
        gs = (gb.astype(F32) * inv).astype(BF16)
        sums[8:16, :reach] += dot(dot_nt(up_v, gs).astype(BF16), p)
        delta = jnp.sum(gb.astype(F32) * output, axis=1, keepdims=True)
        ds = (e * (dweights - delta)).astype(BF16)
        dmixed = dot(ds, kext[:reach, :])
        row_scale = inv * SCALE
        dq = (dmixed[:, :tok] * row_scale).astype(BF16)
        qs = (qb.astype(F32) * row_scale).astype(BF16)
        ob = output.astype(BF16)
        sums[0:8, :reach] += dot(dot_nt(up_k, qs).astype(BF16), ds)
        bk += dot(jnp.transpose(dmixed[:, tok:])[16:24].astype(BF16), qs)
        bv += dot(jnp.transpose(mixed[:, tok:])[24:32].astype(BF16), gs)
        bq += dot(low_q[:, b * BLOCK:(b + 1) * BLOCK], dq)
        ao += dot(low_o[:, b * BLOCK:(b + 1) * BLOCK], ob)
        low_dq = dot_nt(up_q, dq)
        out_red = dot_nt(down, ob)
        pair = jnp.concatenate([low_dq, out_red], axis=0)
        pairs += [pair[:, i * tok:(i + 1) * tok] for i in range(per)]
    for p in range(peers):
        at = lead + p * tok
        own = jnp.concatenate([pairs[p], sums[:, at:at + tok]], axis=0)
        emit(p, own, sums[:, p * tok:(p + 1) * tok] if lead else None)
    return jnp.concatenate([bq, bk, bv, ao], axis=0)


def first_kernel(*refs):
    parts, refs = refs[:HALF_HEADS], refs[HALF_HEADS:]
    qu, ku, vu, od, terms, head, low, token_low, queries, grads, kext, vext, sums = refs
    odd, slot = place()
    tok = HEAD_WIDTH
    for peer, part in zip(partners(), parts):
        at = rows_at(peer)
        queries[at, :] = part[:tok, :]
        grads[at, :] = part[tok:2 * tok, :]
        rows = part[2 * tok:2 * tok + 32, :]
        low[peer] = rows
        t = tokens_first(rows.astype(F32)).astype(BF16)
        token_low[at, :] = t
        kext[at, :tok] = part[2 * tok + 32:3 * tok + 32, :]
        vext[at, :tok] = part[3 * tok + 32:, :]
        kext[at, tok:] = t
        vext[at, tok:] = t

    def emit(p, own, previous):
        terms[p] = own

    head[...] = attend(slot + HALF_HEADS * odd, 0, low, qu, ku, vu, od, queries, grads, kext, vext, sums, emit)


def second_kernel(near, *refs):
    parts, refs = refs[:HALF_HEADS], refs[HALF_HEADS:]
    cross, low, token_low, first_terms, head_f, qu, ku, vu, od, terms, heads, queries, grads, kext, vext, sums = refs
    odd, slot = place()
    tok = HEAD_WIDTH
    length = token_low.shape[0]
    for peer, part in zip(partners(LATER), parts):
        at = rows_at(peer)
        late = rows_at(peer + HALF_HEADS)
        queries[at, :] = part[:tok, :]
        grads[at, :] = part[tok:2 * tok, :]
        kext[late, :tok] = part[2 * tok:3 * tok, :]
        vext[late, :tok] = part[3 * tok:, :]
    kext[length:, tok:] = token_low[...]
    vext[length:, tok:] = token_low[...]
    for p in range(HALF_HEADS):
        at = slice(p * tok, (p + 1) * tok)
        rows = jnp.concatenate([jnp.zeros((16, tok), F32), cross[p, :16, :].astype(F32)], axis=0)
        t = tokens_first(rows).astype(BF16)
        kext[at, :tok] = cross[p, 16:16 + tok, :]
        vext[at, :tok] = cross[p, 16 + tok:, :]
        kext[at, tok:] = t
        vext[at, tok:] = t
    mine = odd * HALF_HEADS
    other = HALF_HEADS - mine

    def emit(p, own, previous):
        own = own + first_terms[p]
        if near:
            terms[mine + p] = own.astype(BF16)
            terms[other + p] = jnp.concatenate([jnp.zeros((16, tok), F32), previous], axis=0).astype(BF16)
        else:
            terms[p] = jnp.concatenate([own, previous], axis=0).astype(BF16)

    head_s = attend(second_head(slot) + HALF_HEADS * (1 - odd), length, low, qu, ku, vu, od, queries, grads, kext, vext, sums, emit)
    heads[:32, :] = head_f[...]
    heads[32:, :] = head_s


def product_kernel(kind, near, terms, *refs):
    own = jnp.sum(terms[:, :32, :].astype(F32), axis=0)
    mixed = own[16:32]
    if not near:
        mixed = mixed + refs[0][...]
        refs = refs[1:]
    x, pog, heads, *outs = refs
    left = jnp.concatenate([own[0:8], mixed], axis=0).astype(BF16)
    right = own[8:16].astype(BF16)
    wide = x.shape[1] // HEAD_WIDTH
    head = heads[...].astype(BF16)
    odd, slot = place()
    step = 4
    zero = lax.axis_index("dp") == 0

    def put(pair, rows, first, second):
        outs[0][pair, rows, :] = jnp.where(zero, first, second)
        outs[1][pair, rows, :] = jnp.where(zero, second, first)

    for c in range(0, wide, step):
        columns = slice(c * HEAD_WIDTH, (c + step) * HEAD_WIDTH)
        a = jnp.concatenate([dot(left, x[:, columns]), dot(right, pog[:, columns])], axis=0).astype(BF16)
        a = [a[:, i * HEAD_WIDTH:(i + 1) * HEAD_WIDTH] for i in range(step)]
        for i in range(step):
            if kind != "paired":
                outs[0][c + i, :32, :] = a[i]
            elif i % 2 == 0:
                put((c + i) // 2, slice(0, 32), a[i], a[i + 1])
    spots = ((slot, odd), (second_head(slot), 1 - odd))
    per = wide // HALF_HEADS
    share = 64 // per
    if kind == "parts":
        outs[1][...] = jnp.zeros(outs[1].shape, BF16)
        for i, (where, half) in enumerate(spots):
            outs[1][where, pl.ds(pl.multiple_of(32 * half, 32), 32), :] = head[32 * i:32 * i + 32]
        return
    for out in outs:
        out[:, 32:, :] = jnp.zeros((out.shape[0], share, HEAD_WIDTH), BF16)
    for i in range(per):
        where, half = spots[2 * i // per]
        at = where * per + half * (per // 2) + i % (per // 2)
        if kind != "paired":
            outs[0][at, 32:, :] = head[i * share:(i + 1) * share]
        elif i % 2 == 0:
            put(lax.div(at, 2), slice(32, 32 + share), head[i * share:(i + 1) * share], head[(i + 1) * share:(i + 2) * share])


def add_kernel(a, b, out):
    out[...] = (a[...].astype(F32) + b[...].astype(F32)).astype(BF16)


def share_kernel(parts, out):
    summed = jnp.sum(parts[...].astype(F32), axis=0).astype(BF16)
    out[...] = jnp.broadcast_to(summed[None], out.shape)


def finish_kernel(kind, *refs):
    outs = refs[-8:]
    refs = refs[:-8]
    wide = outs[0].shape[1] // HEAD_WIDTH
    per = wide // HALF_HEADS
    zero = lax.axis_index("dp") == 0

    def chunk(c):
        if kind == "paired":
            mine, other = refs[0][c // 2], refs[1][c // 2]
            return jnp.where(zero, mine, other) if c % 2 == 0 else jnp.where(zero, other, mine)
        return refs[0][c]

    head = []
    for c in range(wide):
        rows = chunk(c).astype(F32)
        for i, o in enumerate((0, 2, 4, 7)):
            outs[o][:, c * HEAD_WIDTH:(c + 1) * HEAD_WIDTH] = rows[8 * i:8 * i + 8]
        if kind != "parts":
            head.append(rows[32:])
    for j in range(HALF_HEADS):
        if kind == "parts":
            rows = refs[1][j].astype(F32)
        else:
            rows = jnp.concatenate(head[j * per:(j + 1) * per], axis=0)
        for half in range(2):
            at = (j + half * HALF_HEADS) * HEAD_WIDTH
            for i, o in enumerate((1, 3, 5, 6)):
                outs[o][:, at:at + HEAD_WIDTH] = rows[32 * half + 8 * i:32 * half + 8 * i + 8]


def per_device(
    devices,
    normed_input,
    projection_output_gradient,
    query,
    key,
    value,
    frozen_output_gradient,
    query_down_weight,
    query_up_weight,
    key_down_weight,
    key_up_weight,
    value_down_weight,
    value_up_weight,
    output_down_weight,
    output_up_weight,
):
    x = normed_input[0]
    pog = projection_output_gradient[0]
    tok, width = x.shape
    peers = GROUP // 2 // tok
    count = lax.axis_size("ctx")
    groups = [list(range(s, s + peers)) for s in range(0, count, peers)]
    down_t = output_down_weight.T
    ahead = [(s, ((s ^ MIRROR) + peers) % count) for s in range(count)]
    behind = [((s + peers) % count, s) for s in range(count)]
    near = count == 2 * peers

    def swap(array):
        return lax.all_to_all(array, "ctx", 0, 0, axis_index_groups=groups)

    cores = lax.axis_size("dp")

    def exchange(parts, orders):
        moved = [parts[0]]
        for k in range(1, peers):
            pairs = [(c * cores + d, (c ^ orders[d % 2][k]) * cores + d) for c in range(count) for d in range(cores)]
            moved.append(lax.ppermute(parts[k], ("ctx", "dp"), pairs))
        return tuple(moved)

    weights = (query_down_weight.T, key_down_weight.T, value_down_weight.T, output_up_weight, down_t)
    sources = (query[0], key[0], value[0], x, pog, frozen_output_gradient[0]) + weights
    packed = call(
        pack_kernel,
        (jax.ShapeDtypeStruct((4 * tok + 32, HEAD_WIDTH), BF16),) * peers
        + (jax.ShapeDtypeStruct((4 * tok, HEAD_WIDTH), BF16),) * peers,
        sources,
        tuple(pltpu.VMEM(source.shape, BF16) for source in sources) + (pltpu.SemaphoreType.DMA((19,)),),
        flops=1 << 28,
        moved=4 << 20,
        far=len(sources),
        limit=VMEM_PACK,
    )
    firsts, seconds = packed[:peers], packed[peers:]
    firsts = (call(keep_kernel, jax.ShapeDtypeStruct(firsts[0].shape, BF16), firsts[:1]),) + tuple(firsts[1:])
    firsts = exchange(firsts, ORDERS)
    cross = call(
        assemble_kernel,
        jax.ShapeDtypeStruct((peers, 2 * tok + 16, HEAD_WIDTH), BF16),
        firsts,
        moved=2 << 20,
    )
    cross = lax.ppermute(cross, "ctx", ahead)
    seconds = exchange(seconds, LATER)
    length = peers * tok
    ups = (query_up_weight, key_up_weight, value_up_weight, down_t)

    def scratch(keys):
        return (
            pltpu.VMEM((length, HEAD_WIDTH), BF16),
            pltpu.VMEM((length, HEAD_WIDTH), BF16),
            pltpu.VMEM((keys, 2 * HEAD_WIDTH), BF16),
            pltpu.VMEM((keys, 2 * HEAD_WIDTH), BF16),
            pltpu.VMEM((16, keys), F32),
        )

    pairs = length * length
    first_terms, head_f, low, low_tokens = call(
        first_kernel,
        (
            jax.ShapeDtypeStruct((peers, 32, HEAD_WIDTH), F32),
            jax.ShapeDtypeStruct((32, HEAD_WIDTH), F32),
            jax.ShapeDtypeStruct((peers, 32, HEAD_WIDTH), BF16),
            jax.ShapeDtypeStruct((length, HEAD_WIDTH), BF16),
        ),
        firsts + ups,
        scratch(length),
        flops=pairs * 6 * 256,
        moved=3 << 20,
        exps=pairs // 2,
    )
    terms, heads = call(
        functools.partial(second_kernel, near),
        (
            jax.ShapeDtypeStruct((count, 32, HEAD_WIDTH) if near else (peers, 48, HEAD_WIDTH), BF16),
            jax.ShapeDtypeStruct((64, HEAD_WIDTH), F32),
        ),
        seconds + (cross, low, low_tokens, first_terms, head_f) + ups,
        scratch(2 * length),
        flops=3 * pairs * 6 * 256,
        moved=3 << 20,
        exps=3 * pairs // 2,
    )
    if near:
        back = ()
        terms = lax.all_to_all(terms, "ctx", 0, 0)
    else:
        terms = swap(terms)
        back = (lax.ppermute(jnp.sum(terms[:, 32:, :].astype(F32), axis=0), "ctx", behind),)
    wide = width // HEAD_WIDTH
    share = HALF_HEADS * 64 // devices
    direct = devices == wide and share % 16 == 0
    paired = direct and lax.axis_size("dp") == 2
    kind = "paired" if paired else "whole" if direct else "parts"
    other_core = [(0, 1), (1, 0)]
    if paired:
        shapes = (jax.ShapeDtypeStruct((count, 32 + share, HEAD_WIDTH), BF16),) * 2
    elif direct:
        shapes = (jax.ShapeDtypeStruct((wide, 32 + share, HEAD_WIDTH), BF16),)
    else:
        shapes = (
            jax.ShapeDtypeStruct((wide, 32, HEAD_WIDTH), BF16),
            jax.ShapeDtypeStruct((HALF_HEADS, 64, HEAD_WIDTH), BF16),
        )
    parts = call(
        functools.partial(product_kernel, kind, near),
        shapes,
        (terms,) + back + (x, pog, heads),
        flops=2 * 32 * tok * width,
        moved=3 << 20,
    )
    rows = [wide * 32 // devices, share]
    if paired:
        theirs = lax.ppermute(parts[1], "dp", other_core)
        parts = call(add_kernel, shapes[0], (parts[0], theirs), moved=1 << 20)
        parts = lax.all_to_all(parts, "ctx", 0, 0)
    else:
        if direct:
            parts = parts[0]
        else:
            parts = jnp.concatenate(
                [part.reshape(devices, n, HEAD_WIDTH) for part, n in zip(parts, rows)], axis=1)
        parts = lax.all_to_all(parts, ("ctx", "dp"), 0, 0)
    shared = call(
        share_kernel,
        jax.ShapeDtypeStruct(parts.shape, BF16),
        (parts,),
        moved=1 << 20,
    )
    if paired:
        mine = lax.all_to_all(shared, "ctx", 0, 0)
        gathered = (mine, lax.ppermute(mine, "dp", other_core))
    else:
        gathered = (lax.all_to_all(shared, ("ctx", "dp"), 0, 0),)
    if not direct:
        gathered = (
            gathered[0][:, :rows[0]].reshape(wide, 32, HEAD_WIDTH),
            gathered[0][:, rows[0]:].reshape(HALF_HEADS, 64, HEAD_WIDTH),
        )
    narrow = SHIFT_HEADS * HEAD_WIDTH
    columns = (width, narrow, width, narrow, width, narrow, narrow, width)
    outs = call(
        functools.partial(finish_kernel, kind),
        tuple(jax.ShapeDtypeStruct((ADAPTER_RANK, n), F32) for n in columns),
        gathered,
        moved=2 << 20,
    )
    return tuple(out.T if i in (0, 2, 4, 6) else out for i, out in enumerate(outs))


def solution(mesh):
    placed = (P("dp", "ctx", None),) * 6 + (P(),) * 8
    return jax.shard_map(
        functools.partial(per_device, mesh.size),
        mesh=mesh,
        in_specs=placed,
        out_specs=(P(),) * 8,
        check_vma=False,
    )
```
